32 devices in a mesh: chan: 16 (over z, x, core), tm: 2 (over y).
Axes of the slice: x: 2, y: 2, z: 4, core: 2. Of those that a mesh axis runs over, the one named last changes fastest.
Arguments:
- records: bfloat16 [1024, 65536], P('chan', 'tm'), may hold values from -6 to 6
- coords: int32 [2, 1024], P(None, 'chan'), may hold values from 0 to 1023
- bins: int32 [256], replicated, may hold values from 1 to 1023
- slow_index: int32 [2, 2048], replicated, may hold values from -32 to 32
Outputs:
- beam_power: float32 [2048, 256], P('tm', 'chan')
The draws below stay inside these ranges and needn't reach their ends.
All inputs are finite; a program needn't handle non-finite values.
Results may differ from the reference program's by a relative error of at most 0.0011.
Values may be sent and summed in bfloat16 or wider, within the bound.
A program may use at most 64 MiB of HBM per device.

```python
import math
import jax
import jax.numpy as jnp
from jax import lax

W = 2048
F = 256
S = 2048
CHANNELS = 1024
SAMPLES = 65536


def touch_ends(result, rng, low, top_value):
    longest = result.shape.index(max(result.shape))
    spots = []
    for shift in (0, 1):
        where = [jax.random.randint(jax.random.fold_in(rng, axis), (), 0, length) for axis, length in enumerate(result.shape)]
        where[longest] = (where[longest] + shift) % result.shape[longest]
        spots.append(tuple(where))
    return result.at[spots[0]].set(low).at[spots[1]].set(top_value)


def shard_levels(own_key, extent, shards, smallest, largest):
    loudness, own = 1.0, jax.random.fold_in(own_key, 6)
    for dim, parts in shards:
        draws = jnp.exp(jax.random.uniform(jax.random.fold_in(own, dim), (parts,), jnp.float32, smallest / len(shards), largest / len(shards)))
        loudness = loudness * jnp.repeat(draws, extent[dim] // parts).reshape([-1 if axis == dim else 1 for axis in range(len(extent))])
    return loudness


def centred(stream_key, dims, scale, most, split=(), held_as=jnp.bfloat16):
    level = shard_levels(stream_key, dims, split, -0.22, 0.18) if split else 1.0
    result = jax.random.normal(stream_key, dims, jnp.float32) * scale * level
    return jnp.minimum(jnp.maximum(result, -most), most).astype(held_as)


def setup_inputs(seed: int = 0) -> dict:
    key_list = jax.random.split(jax.random.key(seed), 5)
    return {
        "records": centred(key_list[0], (CHANNELS, SAMPLES), 1.0, 6.0, ((0, 16), (1, 2))),
        "coords": touch_ends(jax.random.randint(key_list[1], (2, CHANNELS), 0, 1024), jax.random.fold_in(key_list[1], 1), 0, 1023).astype(jnp.int32),
        "bins": touch_ends(jax.random.randint(key_list[2], (F,), 1, W // 2), jax.random.fold_in(key_list[2], 1), 1, (W // 2) - 1).astype(jnp.int32),
        "slow_index": touch_ends(jax.random.randint(key_list[3], (2, S), -32, 33), jax.random.fold_in(key_list[3], 1), -32, 32).astype(jnp.int32),
    }


def taper_table(bins, width):
    offsets = jnp.arange(width, dtype=jnp.int32)
    turns = jnp.remainder(bins[None, :] * offsets[:, None], width).astype(jnp.float32) * (2.0 * math.pi / width)
    taper = 0.5 - 0.5 * jnp.cos(offsets.astype(jnp.float32) * (2.0 * math.pi / width))
    weight = (taper * math.sqrt(8.0 / (3.0 * width)))[:, None]
    table = jnp.stack([weight * jnp.cos(turns), -weight * jnp.sin(turns)], axis=-1)
    return table.reshape(width, -1).astype(jnp.bfloat16)

def replica_rows(delay, bin_value, width):
    modulus = 5 * width
    phase = jnp.remainder(2 * bin_value * delay, modulus).astype(jnp.float32) * (2.0 * math.pi / modulus)
    return jnp.concatenate([jnp.cos(phase), jnp.sin(phase)], axis=0).astype(jnp.bfloat16)

def reference(records, coords, bins, slow_index):
    channels, samples = records.shape
    hop = W // 2
    snaps = samples // hop
    freq = bins.shape[0]
    slow_count = slow_index.shape[1]
    table = taper_table(bins, W).astype(jnp.float32)
    group = math.gcd(channels, 256)

    def dft_group(piece):
        blocks = piece.astype(jnp.float32).reshape(group, snaps, hop)
        later = jnp.concatenate([blocks[:, 1:], jnp.zeros((group, 1, hop), jnp.float32)], axis=1)
        out = jnp.einsum('cnj,jq->cnq', blocks, table[:hop], precision=lax.Precision.HIGHEST)
        out = out + jnp.einsum('cnj,jq->cnq', later, table[hop:], precision=lax.Precision.HIGHEST)
        return out.astype(jnp.bfloat16)
    spectra = lax.map(dft_group, records.reshape(channels // group, group, samples))
    spectra = spectra.reshape(channels, snaps, freq, 2).transpose(2, 0, 1, 3)
    delay = slow_index[0][:, None] * coords[0][None, :] + slow_index[1][:, None] * coords[1][None, :]

    def one_bin(item):
        bin_value, piece = item
        replica = replica_rows(delay, bin_value, W).astype(jnp.float32)
        flat = piece.astype(jnp.float32).reshape(channels, snaps * 2)
        prod = jnp.dot(replica, flat, precision=lax.Precision.HIGHEST).reshape(2, slow_count, snaps, 2)
        real_part = prod[0, :, :, 0] + prod[1, :, :, 1]
        imag_part = prod[0, :, :, 1] - prod[1, :, :, 0]
        return lax.optimization_barrier(jnp.sum(real_part * real_part + imag_part * imag_part, axis=1)) / (channels * snaps)
    powers = lax.map(one_bin, (bins, spectra))
    return powers.T
```

```python
import functools
import math

import jax
import jax.numpy as jnp
import numpy as np
from jax import lax
from jax.experimental import pallas as pl
from jax.experimental.pallas import tpu as pltpu
from jax.sharding import PartitionSpec as P

W = 2048
REACH = 32
LANES = 128
GROUP = 8


def shifted(block, axis, distance):
    devices = range(lax.axis_size(axis))
    route = [(i - distance, i) for i in devices if i - distance in devices]
    return lax.ppermute(block, axis, route)


def taper_table(bins, width):
    offsets = jnp.arange(width, dtype=jnp.int32)
    turns = jnp.remainder(bins[None, :] * offsets[:, None], width).astype(jnp.float32) * (
        2.0 * math.pi / width
    )
    taper = 0.5 - 0.5 * jnp.cos(offsets.astype(jnp.float32) * (2.0 * math.pi / width))
    weight = (taper * math.sqrt(8.0 / (3.0 * width)))[:, None]
    table = jnp.stack([weight * jnp.cos(turns), -weight * jnp.sin(turns)], axis=-1)
    return table.reshape(width, -1).astype(jnp.bfloat16)


def circle_fit():
    u = 0.125 * (1.0 - np.cos(math.pi * (np.arange(400) + 0.5) / 400))
    t = np.sqrt(u)
    powers = u[:, None] ** np.arange(6)[None, :]
    scaled = powers * (4.0 ** np.arange(6))
    cos_fit = np.linalg.lstsq(scaled, np.cos(2 * math.pi * t), rcond=None)[0]
    sin_fit = np.linalg.lstsq(scaled, np.sin(2 * math.pi * t) / t, rcond=None)[0]
    back = 4.0 ** np.arange(6)
    return [float(v) for v in cos_fit * back], [float(v) for v in sin_fit * back]


COS_FIT, SIN_FIT = circle_fit()


def horner(u, fit):
    total = jnp.full_like(u, fit[-1])
    for value in fit[-2::-1]:
        total = total * u + value
    return total


def circle(t):
    t = t - jnp.floor(t + 0.5)
    u = t * t
    return horner(u, COS_FIT), t * horner(u, SIN_FIT)


def grid_rows(slow_index):
    first, second = slow_index[0], slow_index[1]
    low0, low1 = first < 0, second < 0
    a0, a1 = jnp.abs(first), jnp.abs(second)
    quad = jnp.where(low0 == low1, 0, 2) + low0.astype(jnp.int32)
    inner = quad * REACH * REACH + (a0 - 1) * REACH + a1 - 1
    base = 4 * REACH * REACH
    on_second = base + low1.astype(jnp.int32) * REACH + a1 - 1
    on_first = base + (2 + low0.astype(jnp.int32)) * REACH + a0 - 1
    return jnp.where(
        a0 == 0,
        jnp.where(a1 == 0, base + 4 * REACH, on_second),
        jnp.where(a1 == 0, on_first, inner),
    )


def product(rows, columns):
    return lax.dot_general(
        rows, columns, (((1,), (1,)), ((), ())), preferred_element_type=jnp.float32
    )


def beam_kernel(
    scale, bins_ref, pick_ref, pos_ref, recv_ref, out_ref,
    xt, xj, c0, s0, c1, s1, ra, rb, grid_power,
):
    slots, tm_count, chan_count, tiles, _ = recv_ref.shape
    per_dev = slots // 2
    half = LANES // 2
    side = tm_count * 2 * tiles
    modulus = 5 * W // 2
    lane = lax.broadcasted_iota(jnp.int32, (1, LANES), 1)
    steps = (lax.broadcasted_iota(jnp.int32, (REACH, 1), 0) + 1).astype(jnp.float32)

    def one_bin(f, _):
        bin_value = bins_ref[f].astype(jnp.float32)
        for axis, cos_ref, sin_ref in ((0, c0, s0), (1, c1, s1)):
            turn = pos_ref[axis : axis + 1, :].astype(jnp.float32) * bin_value
            turn = (turn - modulus * jnp.floor(turn * (1.0 / modulus))) * (1.0 / modulus)
            turn = turn - jnp.floor(turn + 0.5)
            cosine, sine = circle(turn * steps)
            cos_ref[...] = cosine
            sin_ref[...] = sine
        for p in range(2):
            for t in range(tm_count):
                for m in range(chan_count // 2):
                    left = recv_ref[2 * f + p, t, 2 * m].astype(jnp.float32)
                    right = recv_ref[2 * f + p, t, 2 * m + 1].astype(jnp.float32)
                    even = jnp.where(lane < half, left, pltpu.roll(right, half, 1))
                    odd = jnp.where(lane < half, pltpu.roll(left, half, 1), right)
                    for parity, value in enumerate((even, odd)):
                        row = (t * 2 + parity) * tiles
                        cols = slice(m * LANES, (m + 1) * LANES)
                        xt[p * side + row : p * side + row + tiles, cols] = value.astype(xt.dtype)
                        q = 1 - p
                        value = value if p else -value
                        xj[q * side + row : q * side + row + tiles, cols] = value.astype(xj.dtype)

        def put(row, values):
            total = jnp.sum(values * values, axis=1, keepdims=True)
            rows = pl.ds(row, values.shape[0])
            grid_power[rows, :] = jnp.where(lane == f, total, grid_power[rows, :])

        def one_group(g, _):
            for k in range(GROUP):
                cos_row = c0[pl.ds(g * GROUP + k, 1), :]
                sin_row = s0[pl.ds(g * GROUP + k, 1), :]
                cosines, sines = c1[...], s1[...]
                at = 2 * REACH * k
                ra[at : at + REACH, :] = (cos_row * cosines).astype(ra.dtype)
                ra[at + REACH : at + 2 * REACH, :] = (sin_row * sines).astype(ra.dtype)
                rb[at : at + REACH, :] = (sin_row * cosines).astype(rb.dtype)
                rb[at + REACH : at + 2 * REACH, :] = (cos_row * sines).astype(rb.dtype)
            da = product(ra[...], xt[...])
            db = product(rb[...], xj[...])
            for k in range(GROUP):
                at = 2 * REACH * k
                cc, ss = da[at : at + REACH], da[at + REACH : at + 2 * REACH]
                sc, cs = db[at : at + REACH], db[at + REACH : at + 2 * REACH]
                even_same, even_other = cc - ss, cc + ss
                odd_same, odd_other = sc + cs, sc - cs
                row = pl.multiple_of((g * GROUP + k) * REACH, REACH)
                put(row, even_same + odd_same)
                put(row + REACH * REACH, even_same - odd_same)
                put(row + 2 * REACH * REACH, even_other + odd_other)
                put(row + 3 * REACH * REACH, even_other - odd_other)
            return 0

        lax.fori_loop(0, REACH // GROUP, one_group, 0)
        ra[0:REACH, :] = c1[...].astype(ra.dtype)
        ra[REACH : 2 * REACH, :] = c0[...].astype(ra.dtype)
        ra[2 * REACH : 2 * REACH + 16, :] = jnp.ones((16, ra.shape[1]), ra.dtype)
        rb[0:REACH, :] = s1[...].astype(rb.dtype)
        rb[REACH : 2 * REACH, :] = s0[...].astype(rb.dtype)
        da = product(ra[0 : 2 * REACH + 16, :], xt[...])
        db = product(rb[0 : 2 * REACH, :], xj[...])
        base = 4 * REACH * REACH
        for k in range(2):
            rows = slice(k * REACH, (k + 1) * REACH)
            put(base + 2 * k * REACH, da[rows] + db[rows])
            put(base + (2 * k + 1) * REACH, da[rows] - db[rows])
        put(base + 4 * REACH, da[2 * REACH :])
        return 0

    lax.fori_loop(0, per_dev, one_bin, 0)

    def pick(block, _):
        start = pl.multiple_of(block * 8, 8)
        for k in range(8):
            out_ref[pl.ds(start + k, 1), :] = grid_power[pl.ds(pick_ref[start + k], 1), :] * scale
        return 0

    lax.fori_loop(0, out_ref.shape[0] // 8, pick, 0)


def beam(received, my_bins, positions, slow_index, scale):
    _, tm_count, chan_count, tiles, _ = received.shape
    channels = positions.shape[1]
    columns = 4 * tm_count * tiles
    half_rows = 2 * REACH * GROUP
    vmem = pl.BlockSpec(memory_space=pltpu.VMEM)
    smem = pl.BlockSpec(memory_space=pltpu.SMEM)
    table = pltpu.VMEM((REACH, channels), jnp.float32)
    return pl.pallas_call(
        functools.partial(beam_kernel, scale),
        out_shape=jax.ShapeDtypeStruct((slow_index.shape[1], LANES), jnp.float32),
        in_specs=[smem, smem, vmem, vmem],
        out_specs=vmem,
        scratch_shapes=[
            pltpu.VMEM((columns, channels), jnp.bfloat16),
            pltpu.VMEM((columns, channels), jnp.bfloat16),
            table, table, table, table,
            pltpu.VMEM((half_rows, channels), jnp.bfloat16),
            pltpu.VMEM((half_rows, channels), jnp.bfloat16),
            pltpu.VMEM((4 * REACH * REACH + 4 * REACH + 16, LANES), jnp.float32),
        ],
        compiler_params=pltpu.CompilerParams(vmem_limit_bytes=48 * 2**20),
        cost_estimate=pl.CostEstimate(
            flops=16 * REACH * REACH * columns * channels * my_bins.shape[0],
            bytes_accessed=received.size * 2,
            transcendentals=0,
        ),
    )(my_bins, grid_rows(slow_index), positions, received)


def shards(records, coords, bins, slow_index):
    ch_dev, local_samples = records.shape
    hop = W // 2
    snaps_dev = local_samples // hop
    chan_count = lax.axis_size("chan")
    tm_count = lax.axis_size("tm")
    channels = ch_dev * chan_count
    freq = bins.shape[0]
    scale = 1.0 / (channels * snaps_dev * tm_count)
    table = taper_table(bins, W)
    blocks = records.reshape(ch_dev, snaps_dev, hop)
    following = shifted(records[:, :hop], "tm", -1)
    first = jnp.einsum("cnj,jq->qnc", blocks, table[:hop], preferred_element_type=jnp.float32)
    second = jnp.einsum(
        "cnj,jq->qnc", blocks[:, 1:], table[hop:], preferred_element_type=jnp.float32
    )
    tail = jnp.einsum("cj,jq->qc", following, table[hop:], preferred_element_type=jnp.float32)
    second = jnp.concatenate([second, tail[:, None, :]], axis=1)
    spectra = (first + second).astype(jnp.bfloat16).reshape(2 * freq, snaps_dev * ch_dev)
    positions = lax.all_gather(coords, "chan", axis=1, tiled=True)
    received = lax.all_to_all(
        lax.all_to_all(spectra, "chan", split_axis=0, concat_axis=1, tiled=True),
        "tm",
        split_axis=0,
        concat_axis=1,
        tiled=True,
    )
    per_dev = freq // (chan_count * tm_count)
    tiles = snaps_dev * ch_dev // LANES
    received = received.reshape(2 * per_dev, tm_count, chan_count, tiles, LANES)
    bin_base = (lax.axis_index("chan") * tm_count + lax.axis_index("tm")) * per_dev
    my_bins = lax.dynamic_slice_in_dim(bins, bin_base, per_dev, 0)
    whole = beam(received, my_bins, positions, slow_index, scale)[:, :per_dev]
    return lax.all_to_all(whole, "tm", split_axis=0, concat_axis=1, tiled=True)


def solution(mesh):
    return jax.shard_map(
        shards,
        mesh=mesh,
        in_specs=(P("chan", "tm"), P(None, "chan"), P(), P()),
        out_specs=P("tm", "chan"),
        check_vma=False,
    )
```

```python
import functools
import math

import jax
import jax.numpy as jnp
import numpy as np
from jax import lax
from jax.experimental import pallas as pl
from jax.experimental.pallas import tpu as pltpu
from jax.sharding import PartitionSpec as P

W = 2048
REACH = 32
LANES = 128
GROUP = 8
CHUNKS = 4


def circle_fit():
    u = 0.125 * (1.0 - np.cos(math.pi * (np.arange(400) + 0.5) / 400))
    t = np.sqrt(u)
    powers = u[:, None] ** np.arange(6)[None, :]
    scaled = powers * (4.0 ** np.arange(6))
    cos_fit = np.linalg.lstsq(scaled, np.cos(2 * math.pi * t), rcond=None)[0]
    sin_fit = np.linalg.lstsq(scaled, np.sin(2 * math.pi * t) / t, rcond=None)[0]
    back = 4.0 ** np.arange(6)
    return [float(v) for v in cos_fit * back], [float(v) for v in sin_fit * back]


COS_FIT, SIN_FIT = circle_fit()


def horner(u, fit):
    total = jnp.full_like(u, fit[-1])
    for value in fit[-2::-1]:
        total = total * u + value
    return total


def circle(t):
    t = t - jnp.floor(t + 0.5)
    u = t * t
    return horner(u, COS_FIT), t * horner(u, SIN_FIT)


def grid_rows(slow_index):
    first, second = slow_index[0], slow_index[1]
    low0, low1 = first < 0, second < 0
    a0, a1 = jnp.abs(first), jnp.abs(second)
    quad = jnp.where(low0 == low1, 0, 2) + low0.astype(jnp.int32)
    inner = quad * REACH * REACH + (a0 - 1) * REACH + a1 - 1
    base = 4 * REACH * REACH
    on_second = base + low1.astype(jnp.int32) * REACH + a1 - 1
    on_first = base + (2 + low0.astype(jnp.int32)) * REACH + a0 - 1
    return jnp.where(
        a0 == 0,
        jnp.where(a1 == 0, base + 4 * REACH, on_second),
        jnp.where(a1 == 0, on_first, inner),
    )


def product(rows, columns):
    return lax.dot_general(
        rows, columns, (((1,), (1,)), ((), ())), preferred_element_type=jnp.float32
    )


def kernel(
    scale, tm_count, chan_count, bins_ref, pick_ref, bin_rows, coords_ref, records_ref, out_ref,
    blocks, table, stage, send, recv, digits, all_digits, positions,
    xt, xj, c0, s0, c1, s1, ra, rb, grid_power,
    load_sem, halo_sems, digit_sems, send_sem, recv_sems,
):
    devices = tm_count * chan_count
    chunks, _, chunk_rows, _ = recv.shape
    ch_dev, local_samples = records_ref.shape
    hop = W // 2
    snaps = local_samples // hop
    tiles = snaps * ch_dev // LANES
    freq_rows = bin_rows.shape[0]
    per_dev = bins_ref.shape[0]
    per_chunk = per_dev // chunks
    half = LANES // 2
    side = tm_count * 2 * tiles
    my_chan, my_tm = lax.axis_index("chan"), lax.axis_index("tm")
    me = my_chan * tm_count + my_tm
    lane = lax.broadcasted_iota(jnp.int32, (1, LANES), 1)
    mesh_id = pl.DeviceIdType.MESH

    barrier = pltpu.get_barrier_semaphore()

    def greet(j, _):
        other = lax.rem(me + j, devices)
        pl.semaphore_signal(
            barrier,
            inc=1,
            device_id=(lax.div(other, tm_count), lax.rem(other, tm_count)),
            device_id_type=mesh_id,
        )
        return 0

    lax.fori_loop(1, devices, greet, 0)

    def load(n, _):
        pltpu.make_async_copy(
            records_ref.at[:, pl.ds(pl.multiple_of(n * hop, hop), hop)],
            blocks.at[pl.ds(pl.multiple_of(n * ch_dev, ch_dev), ch_dev), :],
            load_sem,
        ).start()
        return 0

    lax.fori_loop(0, snaps, load, 0)
    digits[...] = jnp.zeros_like(digits)
    for axis in range(2):
        values = coords_ref[axis : axis + 1, :].astype(jnp.float32)
        high = jnp.floor(values * (1.0 / 32.0))
        digits[2 * axis : 2 * axis + 1, :] = high.astype(digits.dtype)
        digits[2 * axis + 1 : 2 * axis + 2, :] = (values - 32.0 * high).astype(digits.dtype)
    all_digits[my_chan] = digits[...]
    pl.semaphore_wait(barrier, devices - 1)

    halo = pltpu.make_async_remote_copy(
        src_ref=records_ref.at[:, 0:hop],
        dst_ref=blocks.at[snaps * ch_dev : (snaps + 1) * ch_dev, :],
        send_sem=halo_sems.at[0],
        recv_sem=halo_sems.at[1],
        device_id=(my_chan, lax.rem(my_tm + tm_count - 1, tm_count)),
        device_id_type=mesh_id,
    )
    halo.start()

    def tell(j, _):
        pltpu.make_async_remote_copy(
            src_ref=digits,
            dst_ref=all_digits.at[my_chan],
            send_sem=digit_sems.at[0],
            recv_sem=digit_sems.at[1],
            device_id=(lax.rem(my_chan + j, chan_count), my_tm),
            device_id_type=mesh_id,
        ).start()
        return 0

    lax.fori_loop(1, chan_count, tell, 0)

    offset = lax.broadcasted_iota(jnp.int32, (1, W), 1).astype(jnp.float32) * (1.0 / W)
    weight = (0.5 - 0.5 * circle(offset)[0]) * math.sqrt(8.0 / (3.0 * W))
    quarter = lax.rem(lax.broadcasted_iota(jnp.int32, (16, 1), 0), 2).astype(jnp.float32) * 0.25

    def table_rows(r, _):
        rows = pl.ds(pl.multiple_of(r * 16, 16), 16)
        turn = bin_rows[rows, :].astype(jnp.float32) * offset + quarter
        turn = turn - jnp.floor(turn + 0.5)
        table[rows, :] = (weight * horner(turn * turn, COS_FIT)).astype(table.dtype)
        return 0

    lax.fori_loop(0, freq_rows // 16, table_rows, 0)

    whole = blocks.at[0 : snaps * ch_dev, :]
    pltpu.make_async_copy(whole, whole, load_sem).wait()
    halo.wait()
    tail = blocks[snaps * ch_dev :, :]
    blocks[snaps * ch_dev :, :] = jnp.where(my_tm == tm_count - 1, jnp.zeros_like(tail), tail)

    def transform(i, _):
        start = pl.multiple_of(i * 2 * LANES, 2 * LANES)
        here = blocks[pl.ds(start, 2 * LANES), :]
        after = blocks[pl.ds(start + ch_dev, 2 * LANES), :]
        out = product(table[:, :hop], here) + product(table[:, hop:], after)
        for k in range(2):
            rows = pl.ds(2 * i + k, freq_rows, stride=tiles)
            stage[rows, :] = out[:, k * LANES : (k + 1) * LANES]
        return 0

    lax.fori_loop(0, tiles // 2, transform, 0)
    dest_rows = chunks * chunk_rows

    def pack(d, _):
        rows = pl.ds(pl.multiple_of(d * dest_rows, dest_rows), dest_rows)
        send[rows, :] = stage[rows, :].astype(send.dtype)
        return 0

    lax.fori_loop(0, devices, pack, 0)

    def part(k, d):
        start = d * dest_rows + k * chunk_rows
        return pl.ds(pl.multiple_of(start, chunk_rows), chunk_rows)

    def send_chunk(k, _):
        def send_one(j, _):
            other = lax.rem(me + j, devices)
            pltpu.make_async_remote_copy(
                src_ref=send.at[part(k, other), :],
                dst_ref=recv.at[k, me],
                send_sem=send_sem,
                recv_sem=recv_sems.at[k],
                device_id=(lax.div(other, tm_count), lax.rem(other, tm_count)),
                device_id_type=mesh_id,
            ).start()
            return 0

        lax.fori_loop(1, devices, send_one, 0)
        recv[k, me] = send[part(k, me), :]
        return 0

    lax.fori_loop(0, chunks, send_chunk, 0)

    others = all_digits.at[0 : chan_count - 1]
    pltpu.make_async_copy(others, others, digit_sems.at[1]).wait()
    pltpu.make_async_copy(others, others, digit_sems.at[0]).wait()
    for m in range(chan_count // 2):
        left = all_digits[2 * m].astype(jnp.float32)
        right = all_digits[2 * m + 1].astype(jnp.float32)
        both = jnp.where(lane < half, left, right)
        for axis in range(2):
            high, low = both[2 * axis : 2 * axis + 1], both[2 * axis + 1 : 2 * axis + 2]
            positions[axis : axis + 1, m * LANES : (m + 1) * LANES] = 32.0 * high + low

    modulus = 5 * W // 2
    steps = (lax.broadcasted_iota(jnp.int32, (REACH, 1), 0) + 1).astype(jnp.float32)

    def one_bin(k, local, _):
        f = k * per_chunk + local
        bin_value = bins_ref[f].astype(jnp.float32)
        for axis, cos_ref, sin_ref in ((0, c0, s0), (1, c1, s1)):
            turn = positions[axis : axis + 1, :] * bin_value
            turn = (turn - modulus * jnp.floor(turn * (1.0 / modulus))) * (1.0 / modulus)
            turn = turn - jnp.floor(turn + 0.5)
            cosine, sine = circle(turn * steps)
            cos_ref[...] = cosine
            sin_ref[...] = sine
        for p in range(2):
            source_rows = pl.ds(pl.multiple_of((2 * local + p) * tiles, tiles), tiles)
            for t in range(tm_count):
                for m in range(chan_count // 2):
                    left = recv[k, 2 * m * tm_count + t, source_rows, :].astype(jnp.float32)
                    right = recv[k, (2 * m + 1) * tm_count + t, source_rows, :].astype(jnp.float32)
                    even = jnp.where(lane < half, left, pltpu.roll(right, half, 1))
                    odd = jnp.where(lane < half, pltpu.roll(left, half, 1), right)
                    for parity, value in enumerate((even, odd)):
                        row = (t * 2 + parity) * tiles
                        cols = slice(m * LANES, (m + 1) * LANES)
                        xt[p * side + row : p * side + row + tiles, cols] = value.astype(xt.dtype)
                        q = 1 - p
                        value = value if p else -value
                        xj[q * side + row : q * side + row + tiles, cols] = value.astype(xj.dtype)

        def put(row, values):
            total = jnp.sum(values * values, axis=1, keepdims=True)
            rows = pl.ds(row, values.shape[0])
            grid_power[rows, :] = jnp.where(lane == f, total, grid_power[rows, :])

        def one_group(g, _):
            for k in range(GROUP):
                cos_row = c0[pl.ds(g * GROUP + k, 1), :]
                sin_row = s0[pl.ds(g * GROUP + k, 1), :]
                cosines, sines = c1[...], s1[...]
                at = 2 * REACH * k
                ra[at : at + REACH, :] = (cos_row * cosines).astype(ra.dtype)
                ra[at + REACH : at + 2 * REACH, :] = (sin_row * sines).astype(ra.dtype)
                rb[at : at + REACH, :] = (sin_row * cosines).astype(rb.dtype)
                rb[at + REACH : at + 2 * REACH, :] = (cos_row * sines).astype(rb.dtype)
            da = product(ra[...], xt[...])
            db = product(rb[...], xj[...])
            for k in range(GROUP):
                at = 2 * REACH * k
                cc, ss = da[at : at + REACH], da[at + REACH : at + 2 * REACH]
                sc, cs = db[at : at + REACH], db[at + REACH : at + 2 * REACH]
                even_same, even_other = cc - ss, cc + ss
                odd_same, odd_other = sc + cs, sc - cs
                row = pl.multiple_of((g * GROUP + k) * REACH, REACH)
                put(row, even_same + odd_same)
                put(row + REACH * REACH, even_same - odd_same)
                put(row + 2 * REACH * REACH, even_other + odd_other)
                put(row + 3 * REACH * REACH, even_other - odd_other)
            return 0

        lax.fori_loop(0, REACH // GROUP, one_group, 0)
        ra[0:REACH, :] = c1[...].astype(ra.dtype)
        ra[REACH : 2 * REACH, :] = c0[...].astype(ra.dtype)
        ra[2 * REACH : 2 * REACH + 16, :] = jnp.ones((16, ra.shape[1]), ra.dtype)
        rb[0:REACH, :] = s1[...].astype(rb.dtype)
        rb[REACH : 2 * REACH, :] = s0[...].astype(rb.dtype)
        da = product(ra[0 : 2 * REACH + 16, :], xt[...])
        db = product(rb[0 : 2 * REACH, :], xj[...])
        base = 4 * REACH * REACH
        for k in range(2):
            rows = slice(k * REACH, (k + 1) * REACH)
            put(base + 2 * k * REACH, da[rows] + db[rows])
            put(base + (2 * k + 1) * REACH, da[rows] - db[rows])
        put(base + 4 * REACH, da[2 * REACH :])
        return 0

    grid_power[...] = jnp.zeros_like(grid_power)

    def one_chunk(k, _):
        arrived = recv.at[k, 0 : devices - 1]
        pltpu.make_async_copy(arrived, arrived, recv_sems.at[k]).wait()
        lax.fori_loop(0, per_chunk, functools.partial(one_bin, k), 0)
        return 0

    lax.fori_loop(0, chunks, one_chunk, 0)

    def pick(block, _):
        start = pl.multiple_of(block * 8, 8)
        for k in range(8):
            out_ref[pl.ds(start + k, 1), :] = grid_power[pl.ds(pick_ref[start + k], 1), :] * scale
        return 0

    lax.fori_loop(0, out_ref.shape[0] // 8, pick, 0)
    sent = send.at[0 : (devices - 1) * dest_rows, :]
    pltpu.make_async_copy(sent, sent, send_sem).wait()


def shards(records, coords, bins, slow_index):
    ch_dev, local_samples = records.shape
    hop = W // 2
    snaps = local_samples // hop
    chan_count = lax.axis_size("chan")
    tm_count = lax.axis_size("tm")
    devices = chan_count * tm_count
    channels = ch_dev * chan_count
    freq = bins.shape[0]
    per_dev = freq // devices
    chunks = math.gcd(per_dev, CHUNKS)
    tiles = snaps * ch_dev // LANES
    chunk_rows = 2 * per_dev * tiles // chunks
    columns = 4 * tm_count * tiles
    half_rows = 2 * REACH * GROUP
    scale = 1.0 / (channels * snaps * tm_count)
    bin_base = (lax.axis_index("chan") * tm_count + lax.axis_index("tm")) * per_dev
    my_bins = lax.dynamic_slice_in_dim(bins, bin_base, per_dev, 0)
    bin_rows = jnp.repeat(bins, 2)[:, None]
    twice = jnp.concatenate([coords] * (LANES // ch_dev), axis=1)
    vmem = pl.BlockSpec(memory_space=pltpu.VMEM)
    smem = pl.BlockSpec(memory_space=pltpu.SMEM)
    angles = pltpu.VMEM((REACH, channels), jnp.float32)
    picked = pl.pallas_call(
        functools.partial(kernel, scale, tm_count, chan_count),
        out_shape=jax.ShapeDtypeStruct((slow_index.shape[1], LANES), jnp.float32),
        in_specs=[smem, smem, vmem, vmem, pl.BlockSpec(memory_space=pl.ANY)],
        out_specs=vmem,
        scratch_shapes=[
            pltpu.VMEM(((snaps + 1) * ch_dev, hop), jnp.bfloat16),
            pltpu.VMEM((2 * freq, W), jnp.bfloat16),
            pltpu.VMEM((2 * freq * tiles, LANES), jnp.float32),
            pltpu.VMEM((2 * freq * tiles, LANES), jnp.bfloat16),
            pltpu.VMEM((chunks, devices, chunk_rows, LANES), jnp.bfloat16),
            pltpu.VMEM((16, LANES), jnp.bfloat16),
            pltpu.VMEM((chan_count, 16, LANES), jnp.bfloat16),
            pltpu.VMEM((2, channels), jnp.float32),
            pltpu.VMEM((columns, channels), jnp.bfloat16),
            pltpu.VMEM((columns, channels), jnp.bfloat16),
            angles, angles, angles, angles,
            pltpu.VMEM((half_rows, channels), jnp.bfloat16),
            pltpu.VMEM((half_rows, channels), jnp.bfloat16),
            pltpu.VMEM((4 * REACH * REACH + 4 * REACH + 16, LANES), jnp.float32),
            pltpu.SemaphoreType.DMA,
            pltpu.SemaphoreType.DMA((2,)),
            pltpu.SemaphoreType.DMA((2,)),
            pltpu.SemaphoreType.DMA,
            pltpu.SemaphoreType.DMA((chunks,)),
        ],
        compiler_params=pltpu.CompilerParams(
            collective_id=0, has_side_effects=True, vmem_limit_bytes=52 * 2**20
        ),
        cost_estimate=pl.CostEstimate(
            flops=16 * REACH * REACH * columns * channels * per_dev,
            bytes_accessed=records.size * 2,
            transcendentals=0,
        ),
    )(my_bins, grid_rows(slow_index), bin_rows, twice, records)
    return lax.all_to_all(picked[:, :per_dev], "tm", split_axis=0, concat_axis=1, tiled=True)


def solution(mesh):
    return jax.shard_map(
        shards,
        mesh=mesh,
        in_specs=(P("chan", "tm"), P(None, "chan"), P(), P()),
        out_specs=P("tm", "chan"),
        check_vma=False,
    )
```

```python
import functools
import math

import jax
import jax.numpy as jnp
import numpy as np
from jax import lax
from jax.experimental import pallas as pl
from jax.experimental.pallas import tpu as pltpu
from jax.sharding import PartitionSpec as P

W = 2048
REACH = 32
LANES = 128
INNER = 6
OUTER = 2
SPAN = 2 * INNER + 1
TURNS = 2 * OUTER + 1
CHUNKS = 4


def circle_fit():
    u = 0.125 * (1.0 - np.cos(math.pi * (np.arange(400) + 0.5) / 400))
    t = np.sqrt(u)
    powers = u[:, None] ** np.arange(6)[None, :]
    scaled = powers * (4.0 ** np.arange(6))
    cos_fit = np.linalg.lstsq(scaled, np.cos(2 * math.pi * t), rcond=None)[0]
    sin_fit = np.linalg.lstsq(scaled, np.sin(2 * math.pi * t) / t, rcond=None)[0]
    back = 4.0 ** np.arange(6)
    return [float(v) for v in cos_fit * back], [float(v) for v in sin_fit * back]


COS_FIT, SIN_FIT = circle_fit()


def horner(u, fit):
    total = jnp.full_like(u, fit[-1])
    for value in fit[-2::-1]:
        total = total * u + value
    return total


def circle(t):
    t = t - jnp.floor(t + 0.5)
    u = t * t
    return horner(u, COS_FIT), t * horner(u, SIN_FIT)


MAIN = TURNS * 4 * INNER * REACH
FLAT = MAIN + TURNS * 2 * REACH
GRID = FLAT + TURNS * 2 * 8


def grid_rows(slow_index):
    turn = (slow_index[0] + REACH) // SPAN
    inner = slow_index[0] - SPAN * (turn - OUTER)
    second = slow_index[1]
    low0, low1 = (inner < 0).astype(jnp.int32), (second < 0).astype(jnp.int32)
    a0, a1 = jnp.abs(inner), jnp.abs(second)
    quad = jnp.where(low0 == low1, 0, 2) + low0
    main = ((turn * 4 + quad) * INNER + a0 - 1) * REACH + a1 - 1
    on_second = MAIN + (turn * 2 + low1) * REACH + a1 - 1
    on_first = FLAT + (turn * 2 + low0) * 8 + a0
    return jnp.where(a1 == 0, on_first, jnp.where(a0 == 0, on_second, main))


def product(rows, columns):
    return lax.dot_general(
        rows, columns, (((1,), (1,)), ((), ())), preferred_element_type=jnp.float32
    )


def kernel(
    scale, tm_count, chan_count, bins_ref, pick_ref, coords_ref, records_ref, out_ref,
    blocks, table, stage, send, recv, digits, all_digits, positions,
    yt, yj, c0, s0, c1, s1, ra, rb, grid_power, picked, mine, swapped,
    load_sem, halo_sems, digit_sems, send_sems, recv_sems, power_sems,
):
    devices = tm_count * chan_count
    chunks, _, chunk_rows, _ = recv.shape
    ch_dev, local_samples = records_ref.shape
    hop = W // 2
    snaps = local_samples // hop
    tiles = snaps * ch_dev // LANES
    per_dev = bins_ref.shape[0] // devices
    per_chunk = per_dev // chunks
    freq_rows = table.shape[0]
    half = LANES // 2
    side = tm_count * 2 * tiles
    my_chan, my_tm = lax.axis_index("chan"), lax.axis_index("tm")
    me = my_chan * tm_count + my_tm
    lane = lax.broadcasted_iota(jnp.int32, (1, LANES), 1)
    mesh_id = pl.DeviceIdType.MESH

    barrier = pltpu.get_barrier_semaphore()

    def greet(j, _):
        other = lax.rem(me + j, devices)
        pl.semaphore_signal(
            barrier,
            inc=1,
            device_id=(lax.div(other, tm_count), lax.rem(other, tm_count)),
            device_id_type=mesh_id,
        )
        return 0

    lax.fori_loop(1, devices, greet, 0)

    def load(n, _):
        pltpu.make_async_copy(
            records_ref.at[:, pl.ds(pl.multiple_of(n * hop, hop), hop)],
            blocks.at[pl.ds(pl.multiple_of(n * ch_dev, ch_dev), ch_dev), :],
            load_sem,
        ).start()
        return 0

    lax.fori_loop(0, snaps, load, 0)
    digits[...] = jnp.zeros_like(digits)
    for axis in range(2):
        values = coords_ref[axis : axis + 1, :].astype(jnp.float32)
        high = jnp.floor(values * (1.0 / 32.0))
        digits[2 * axis : 2 * axis + 1, 0:ch_dev] = high.astype(digits.dtype)
        digits[2 * axis + 1 : 2 * axis + 2, 0:ch_dev] = (values - 32.0 * high).astype(digits.dtype)
    all_digits[my_chan] = digits[...]
    pl.semaphore_wait(barrier, devices - 1)

    halo = pltpu.make_async_remote_copy(
        src_ref=records_ref.at[:, 0:hop],
        dst_ref=blocks.at[snaps * ch_dev : (snaps + 1) * ch_dev, :],
        send_sem=halo_sems.at[0],
        recv_sem=halo_sems.at[1],
        device_id=(my_chan, lax.rem(my_tm + tm_count - 1, tm_count)),
        device_id_type=mesh_id,
    )
    halo.start()

    def tell(j, _):
        pltpu.make_async_remote_copy(
            src_ref=digits,
            dst_ref=all_digits.at[my_chan],
            send_sem=digit_sems.at[0],
            recv_sem=digit_sems.at[1],
            device_id=(lax.rem(my_chan + j, chan_count), my_tm),
            device_id_type=mesh_id,
        ).start()
        return 0

    lax.fori_loop(1, chan_count, tell, 0)

    offset = lax.broadcasted_iota(jnp.int32, (1, W), 1).astype(jnp.float32) * (1.0 / W)
    weight = (0.5 - 0.5 * circle(offset)[0]) * math.sqrt(8.0 / (3.0 * W))
    row16 = lax.broadcasted_iota(jnp.int32, (16, 1), 0)
    quarter = lax.rem(row16, 2).astype(jnp.float32) * 0.25

    def table_chunk(k):
        def table_rows(r, _):
            values = jnp.zeros((16, 1), jnp.float32)
            for i in range(8):
                b = r * 8 + i
                index = lax.div(b, per_chunk) * per_dev + k * per_chunk + lax.rem(b, per_chunk)
                values = jnp.where(row16 // 2 == i, bins_ref[index].astype(jnp.float32), values)
            turn = values * offset + quarter
            turn = turn - jnp.floor(turn + 0.5)
            rows = pl.ds(pl.multiple_of(r * 16, 16), 16)
            table[rows, :] = (weight * horner(turn * turn, COS_FIT)).astype(table.dtype)
            return 0

        lax.fori_loop(0, freq_rows // 16, table_rows, 0)

    table_chunk(0)
    whole = blocks.at[0 : snaps * ch_dev, :]
    pltpu.make_async_copy(whole, whole, load_sem).wait()
    halo.wait()
    tail = blocks[snaps * ch_dev :, :]
    blocks[snaps * ch_dev :, :] = jnp.where(my_tm == tm_count - 1, jnp.zeros_like(tail), tail)

    def part(d):
        return pl.ds(pl.multiple_of(d * chunk_rows, chunk_rows), chunk_rows)

    def send_chunk(k, _):
        def transform(i, _):
            start = pl.multiple_of(i * 2 * LANES, 2 * LANES)
            here = blocks[pl.ds(start, 2 * LANES), :]
            after = blocks[pl.ds(start + ch_dev, 2 * LANES), :]
            out = product(table[:, :hop], here) + product(table[:, hop:], after)
            for j in range(2):
                rows = pl.ds(2 * i + j, freq_rows, stride=tiles)
                stage[rows, :] = out[:, j * LANES : (j + 1) * LANES]
            return 0

        lax.fori_loop(0, tiles // 2, transform, 0)

        def pack(d, _):
            send[k, part(d), :] = stage[part(d), :].astype(send.dtype)
            return 0

        lax.fori_loop(0, devices, pack, 0)

        def send_one(j, _):
            other = lax.rem(me + j, devices)
            pltpu.make_async_remote_copy(
                src_ref=send.at[k, part(other), :],
                dst_ref=recv.at[k, me],
                send_sem=send_sems.at[k],
                recv_sem=recv_sems.at[k],
                device_id=(lax.div(other, tm_count), lax.rem(other, tm_count)),
                device_id_type=mesh_id,
            ).start()
            return 0

        lax.fori_loop(1, devices, send_one, 0)
        recv[k, me] = send[k, part(me), :]

        @pl.when(k + 1 < chunks)
        def _():
            table_chunk(k + 1)

        return 0

    lax.fori_loop(0, chunks, send_chunk, 0)

    others = all_digits.at[0 : chan_count - 1]
    pltpu.make_async_copy(others, others, digit_sems.at[1]).wait()
    pltpu.make_async_copy(others, others, digit_sems.at[0]).wait()
    for m in range(chan_count // 2):
        left = all_digits[2 * m].astype(jnp.float32)
        right = pltpu.roll(all_digits[2 * m + 1].astype(jnp.float32), half, 1)
        both = jnp.where(lane < half, left, right)
        for axis in range(2):
            high, low = both[2 * axis : 2 * axis + 1], both[2 * axis + 1 : 2 * axis + 2]
            positions[axis : axis + 1, m * LANES : (m + 1) * LANES] = 32.0 * high + low

    modulus = 5 * W // 2
    inner_step = lax.broadcasted_iota(jnp.int32, (8, 1), 0)
    inner_step = jnp.where(inner_step <= INNER, inner_step, SPAN).astype(jnp.float32)
    step = (lax.broadcasted_iota(jnp.int32, (REACH, 1), 0) + 1).astype(jnp.float32)

    def one_bin(k, local, _):
        f = k * per_chunk + local
        bin_value = bins_ref[me * per_dev + f].astype(jnp.float32)
        for axis, steps, cos_ref, sin_ref in ((0, inner_step, c0, s0), (1, step, c1, s1)):
            turn = positions[axis : axis + 1, :] * bin_value
            turn = (turn - modulus * jnp.floor(turn * (1.0 / modulus))) * (1.0 / modulus)
            turn = turn - jnp.floor(turn + 0.5)
            cosine, sine = circle(turn * steps)
            cos_ref[...] = cosine
            sin_ref[...] = sine
        for m in range(chan_count // 2):
            cols = slice(m * LANES, (m + 1) * LANES)
            cos_1, sin_1 = c0[INNER + 1 : INNER + 2, cols], s0[INNER + 1 : INNER + 2, cols]
            spins = [(cos_1, sin_1), (2.0 * cos_1 * cos_1 - 1.0, 2.0 * sin_1 * cos_1)]
            for t in range(tm_count):
                pairs = []
                for p in range(2):
                    rows = pl.ds(pl.multiple_of((2 * local + p) * tiles, tiles), tiles)
                    left = recv[k, 2 * m * tm_count + t, rows, :].astype(jnp.float32)
                    right = recv[k, (2 * m + 1) * tm_count + t, rows, :].astype(jnp.float32)
                    even = jnp.where(lane < half, left, pltpu.roll(right, half, 1))
                    odd = jnp.where(lane < half, pltpu.roll(left, half, 1), right)
                    pairs.append((even, odd))
                for parity in range(2):
                    re, im = pairs[0][parity], pairs[1][parity]
                    turned = [None] * TURNS
                    turned[OUTER] = (re, im)
                    for h, (cosine, sine) in enumerate(spins, 1):
                        cr, si, ci, sr = cosine * re, sine * im, cosine * im, sine * re
                        turned[OUTER + h] = (cr + si, ci - sr)
                        turned[OUTER - h] = (cr - si, ci + sr)
                    for h, (real, imag) in enumerate(turned):
                        top = 2 * side * h + (t * 2 + parity) * tiles
                        low = top + side
                        yt[top : top + tiles, cols] = real.astype(yt.dtype)
                        yt[low : low + tiles, cols] = imag.astype(yt.dtype)
                        yj[top : top + tiles, cols] = imag.astype(yj.dtype)
                        yj[low : low + tiles, cols] = (-real).astype(yj.dtype)

        def put(row, values):
            total = jnp.sum(values * values, axis=1, keepdims=True)
            rows = pl.ds(row, values.shape[0])
            grid_power[rows, :] = jnp.where(lane == f, total, grid_power[rows, :])

        cosines, sines = c1[...], s1[...]
        for l in range(INNER):
            cos_row, sin_row = c0[l + 1 : l + 2, :], s0[l + 1 : l + 2, :]
            at = 2 * REACH * l
            ra[at : at + REACH, :] = (cos_row * cosines).astype(ra.dtype)
            ra[at + REACH : at + 2 * REACH, :] = (sin_row * sines).astype(ra.dtype)
            rb[at : at + REACH, :] = (sin_row * cosines).astype(rb.dtype)
            rb[at + REACH : at + 2 * REACH, :] = (cos_row * sines).astype(rb.dtype)
        edge = 2 * REACH * INNER
        ra[edge : edge + REACH, :] = cosines.astype(ra.dtype)
        rb[edge : edge + REACH, :] = sines.astype(rb.dtype)
        flat = edge + REACH
        ra[flat : flat + 16, :] = jnp.concatenate([c0[...]] * 2, axis=0).astype(ra.dtype)
        rb[flat : flat + 16, :] = jnp.concatenate([s0[...]] * 2, axis=0).astype(rb.dtype)
        for first in range(0, TURNS, 2):
            turns = range(first, min(first + 2, TURNS))
            columns = slice(2 * side * turns[0], 2 * side * (turns[-1] + 1))
            da = product(ra[...], yt[columns, :])
            db = product(rb[...], yj[columns, :])
            for h in turns:
                lanes = slice(2 * side * (h - first), 2 * side * (h - first + 1))
                for l in range(INNER):
                    at = 2 * REACH * l
                    cc, ss = da[at : at + REACH, lanes], da[at + REACH : at + 2 * REACH, lanes]
                    sc, cs = db[at : at + REACH, lanes], db[at + REACH : at + 2 * REACH, lanes]
                    even_same, even_other = cc - ss, cc + ss
                    odd_same, odd_other = sc + cs, sc - cs
                    row, step_rows = (h * 4 * INNER + l) * REACH, INNER * REACH
                    put(row, even_same + odd_same)
                    put(row + step_rows, even_same - odd_same)
                    put(row + 2 * step_rows, even_other + odd_other)
                    put(row + 3 * step_rows, even_other - odd_other)
                even, odd = da[edge:flat, lanes], db[edge:flat, lanes]
                put(MAIN + 2 * h * REACH, even + odd)
                put(MAIN + (2 * h + 1) * REACH, even - odd)
                even, odd = da[flat : flat + 8, lanes], db[flat : flat + 8, lanes]
                put(FLAT + 16 * h, even + odd)
                put(FLAT + 16 * h + 8, even - odd)
        return 0

    grid_power[...] = jnp.zeros_like(grid_power)

    def one_chunk(k, _):
        arrived = recv.at[k, 0 : devices - 1]
        pltpu.make_async_copy(arrived, arrived, recv_sems.at[k]).wait()
        lax.fori_loop(0, per_chunk, functools.partial(one_bin, k), 0)
        return 0

    lax.fori_loop(0, chunks, one_chunk, 0)

    def pick(block, _):
        start = pl.multiple_of(block * 8, 8)
        for k in range(8):
            picked[pl.ds(start + k, 1), :] = grid_power[pl.ds(pick_ref[start + k], 1), :] * scale
        return 0

    lax.fori_loop(0, picked.shape[0] // 8, pick, 0)
    kept = mine.shape[1]
    own = mine.shape[2]
    for t in range(tm_count):
        for b in range(own // LANES):
            start = t * own + b * LANES
            turned = picked[start : start + LANES, :].T
            mine[t, :, b * LANES : (b + 1) * LANES] = turned[:kept, :]
    exchanges = []
    for j in range(1, tm_count):
        other = lax.rem(my_tm + j, tm_count)
        copy = pltpu.make_async_remote_copy(
            src_ref=mine.at[other],
            dst_ref=swapped.at[my_tm],
            send_sem=power_sems.at[0, j - 1],
            recv_sem=power_sems.at[1, j - 1],
            device_id=(my_chan, other),
            device_id_type=mesh_id,
        )
        copy.start()
        exchanges.append(copy)
    swapped[my_tm] = mine[my_tm]
    for copy in exchanges:
        copy.wait()
    out_ref[...] = swapped[...]

    def drain(k, _):
        sent = send.at[k, 0 : (devices - 1) * chunk_rows, :]
        pltpu.make_async_copy(sent, sent, send_sems.at[k]).wait()
        return 0

    lax.fori_loop(0, chunks, drain, 0)


def shards(records, coords, bins, slow_index):
    ch_dev, local_samples = records.shape
    hop = W // 2
    snaps = local_samples // hop
    chan_count = lax.axis_size("chan")
    tm_count = lax.axis_size("tm")
    devices = chan_count * tm_count
    channels = ch_dev * chan_count
    freq = bins.shape[0]
    per_dev = freq // devices
    chunks = math.gcd(per_dev, CHUNKS)
    tiles = snaps * ch_dev // LANES
    chunk_rows = 2 * per_dev * tiles // chunks
    columns = TURNS * 4 * tm_count * tiles
    side_rows = 2 * REACH * INNER + REACH + 16
    kept = 8 * ((per_dev + 7) // 8)
    own = slow_index.shape[1] // tm_count
    scale = 1.0 / (channels * snaps * tm_count)
    vmem = pl.BlockSpec(memory_space=pltpu.VMEM)
    smem = pl.BlockSpec(memory_space=pltpu.SMEM)
    inner_angles = pltpu.VMEM((8, channels), jnp.float32)
    angles = pltpu.VMEM((REACH, channels), jnp.float32)
    power = pl.pallas_call(
        functools.partial(kernel, scale, tm_count, chan_count),
        out_shape=jax.ShapeDtypeStruct((tm_count, kept, own), jnp.float32),
        in_specs=[smem, smem, vmem, pl.BlockSpec(memory_space=pl.ANY)],
        out_specs=vmem,
        scratch_shapes=[
            pltpu.VMEM(((snaps + 1) * ch_dev, hop), jnp.bfloat16),
            pltpu.VMEM((2 * freq // chunks, W), jnp.bfloat16),
            pltpu.VMEM((2 * freq * tiles // chunks, LANES), jnp.float32),
            pltpu.VMEM((chunks, devices * chunk_rows, LANES), jnp.bfloat16),
            pltpu.VMEM((chunks, devices, chunk_rows, LANES), jnp.bfloat16),
            pltpu.VMEM((16, LANES), jnp.bfloat16),
            pltpu.VMEM((chan_count, 16, LANES), jnp.bfloat16),
            pltpu.VMEM((2, channels), jnp.float32),
            pltpu.VMEM((columns, channels), jnp.bfloat16),
            pltpu.VMEM((columns, channels), jnp.bfloat16),
            inner_angles, inner_angles, angles, angles,
            pltpu.VMEM((side_rows, channels), jnp.bfloat16),
            pltpu.VMEM((side_rows, channels), jnp.bfloat16),
            pltpu.VMEM((GRID, LANES), jnp.float32),
            pltpu.VMEM((slow_index.shape[1], LANES), jnp.float32),
            pltpu.VMEM((tm_count, kept, own), jnp.float32),
            pltpu.VMEM((tm_count, kept, own), jnp.float32),
            pltpu.SemaphoreType.DMA,
            pltpu.SemaphoreType.DMA((2,)),
            pltpu.SemaphoreType.DMA((2,)),
            pltpu.SemaphoreType.DMA((chunks,)),
            pltpu.SemaphoreType.DMA((chunks,)),
            pltpu.SemaphoreType.DMA((2, tm_count)),
        ],
        compiler_params=pltpu.CompilerParams(
            collective_id=0, has_side_effects=True, vmem_limit_bytes=52 * 2**20
        ),
        cost_estimate=pl.CostEstimate(
            flops=4 * side_rows * columns * channels * per_dev,
            bytes_accessed=records.size * 2,
            transcendentals=0,
        ),
    )(bins, grid_rows(slow_index), coords, records)
    return power[:, :per_dev, :].reshape(tm_count * per_dev, own).T


def solution(mesh):
    return jax.shard_map(
        shards,
        mesh=mesh,
        in_specs=(P("chan", "tm"), P(None, "chan"), P(), P()),
        out_specs=P("tm", "chan"),
        check_vma=False,
    )
```

```python
import functools
import math

import jax
import jax.numpy as jnp
import numpy as np
from jax import lax
from jax.experimental import pallas as pl
from jax.experimental.pallas import tpu as pltpu
from jax.sharding import PartitionSpec as P

W = 2048
REACH = 32
LANES = 128
INNER = 6
OUTER = 2
SPAN = 2 * INNER + 1
TURNS = 2 * OUTER + 1
CHUNKS = 4


def circle_fit():
    u = 0.125 * (1.0 - np.cos(math.pi * (np.arange(400) + 0.5) / 400))
    t = np.sqrt(u)
    powers = u[:, None] ** np.arange(6)[None, :]
    scaled = powers * (4.0 ** np.arange(6))
    cos_fit = np.linalg.lstsq(scaled, np.cos(2 * math.pi * t), rcond=None)[0]
    sin_fit = np.linalg.lstsq(scaled, np.sin(2 * math.pi * t) / t, rcond=None)[0]
    back = 4.0 ** np.arange(6)
    return [float(v) for v in cos_fit * back], [float(v) for v in sin_fit * back]


COS_FIT, SIN_FIT = circle_fit()


def horner(u, fit):
    total = jnp.full_like(u, fit[-1])
    for value in fit[-2::-1]:
        total = total * u + value
    return total


def circle(t):
    t = t - jnp.floor(t + 0.5)
    u = t * t
    return horner(u, COS_FIT), t * horner(u, SIN_FIT)


SECOND = INNER * REACH
FIRST = SECOND + REACH
SET = 2 * LANES
POINTS = 8 * ((4 * TURNS + 7) // 8)


def grid_place(slow_index):
    first, second = slow_index[0:1, :], slow_index[1:2, :]
    turn = sum((first + REACH >= SPAN * h).astype(jnp.int32) for h in range(1, TURNS))
    inner = first - SPAN * (turn - OUTER)
    low0, low1 = (inner < 0).astype(jnp.int32), (second < 0).astype(jnp.int32)
    a0, a1 = jnp.abs(inner), jnp.abs(second)
    quad = jnp.where(low0 == low1, low0, 2 + low0)
    quad = jnp.where(a0 == 0, low1, jnp.where(a1 == 0, low0, quad))
    lane = jnp.where(a0 == 0, SECOND + a1 - 1, (a0 - 1) * REACH + a1 - 1)
    return turn * 4 + quad, jnp.where(a1 == 0, FIRST + a0, lane)


def product(rows, columns):
    return lax.dot_general(
        rows, columns, (((1,), (1,)), ((), ())), preferred_element_type=jnp.float32
    )


def kernel(
    scale, tm_count, chan_count, bins_ref, slow_ref, coords_ref, records_ref, out_ref,
    blocks, table, stage, send, recv, digits, all_digits, positions,
    yt, yj, c0, s0, c1, s1, sets, dots, power, place, onehot, mine, swapped,
    load_sem, halo_sems, digit_sems, send_sems, recv_sems, power_sems,
):
    devices = tm_count * chan_count
    chunks, _, chunk_rows, _ = recv.shape
    ch_dev, local_samples = records_ref.shape
    hop = W // 2
    snaps = local_samples // hop
    tiles = snaps * ch_dev // LANES
    per_dev = bins_ref.shape[0] // devices
    per_chunk = per_dev // chunks
    freq_rows = table.shape[0]
    half = LANES // 2
    side = tm_count * 2 * tiles
    my_chan, my_tm = lax.axis_index("chan"), lax.axis_index("tm")
    me = my_chan * tm_count + my_tm
    lane = lax.broadcasted_iota(jnp.int32, (1, LANES), 1)
    mesh_id = pl.DeviceIdType.MESH

    barrier = pltpu.get_barrier_semaphore()

    def greet(j, _):
        other = lax.rem(me + j, devices)
        pl.semaphore_signal(
            barrier,
            inc=1,
            device_id=(lax.div(other, tm_count), lax.rem(other, tm_count)),
            device_id_type=mesh_id,
        )
        return 0

    lax.fori_loop(1, devices, greet, 0)

    def load(n, _):
        pltpu.make_async_copy(
            records_ref.at[:, pl.ds(pl.multiple_of(n * hop, hop), hop)],
            blocks.at[pl.ds(pl.multiple_of(n * ch_dev, ch_dev), ch_dev), :],
            load_sem,
        ).start()
        return 0

    lax.fori_loop(0, snaps, load, 0)
    digits[...] = jnp.zeros_like(digits)
    for axis in range(2):
        values = coords_ref[axis : axis + 1, :].astype(jnp.float32)
        high = jnp.floor(values * (1.0 / 32.0))
        digits[2 * axis : 2 * axis + 1, 0:ch_dev] = high.astype(digits.dtype)
        digits[2 * axis + 1 : 2 * axis + 2, 0:ch_dev] = (values - 32.0 * high).astype(digits.dtype)
    all_digits[my_chan] = digits[...]
    pl.semaphore_wait(barrier, devices - 1)

    halo = pltpu.make_async_remote_copy(
        src_ref=records_ref.at[:, 0:hop],
        dst_ref=blocks.at[snaps * ch_dev : (snaps + 1) * ch_dev, :],
        send_sem=halo_sems.at[0],
        recv_sem=halo_sems.at[1],
        device_id=(my_chan, lax.rem(my_tm + tm_count - 1, tm_count)),
        device_id_type=mesh_id,
    )
    halo.start()

    def tell(j, _):
        pltpu.make_async_remote_copy(
            src_ref=digits,
            dst_ref=all_digits.at[my_chan],
            send_sem=digit_sems.at[0],
            recv_sem=digit_sems.at[1],
            device_id=(lax.rem(my_chan + j, chan_count), my_tm),
            device_id_type=mesh_id,
        ).start()
        return 0

    lax.fori_loop(1, chan_count, tell, 0)

    offset = lax.broadcasted_iota(jnp.int32, (1, W), 1).astype(jnp.float32) * (1.0 / W)
    weight = (0.5 - 0.5 * circle(offset)[0]) * math.sqrt(8.0 / (3.0 * W))
    row16 = lax.broadcasted_iota(jnp.int32, (16, 1), 0)
    quarter = lax.rem(row16, 2).astype(jnp.float32) * 0.25

    def table_chunk(k):
        def table_rows(r, _):
            values = jnp.zeros((16, 1), jnp.float32)
            for i in range(8):
                b = r * 8 + i
                index = lax.div(b, per_chunk) * per_dev + k * per_chunk + lax.rem(b, per_chunk)
                values = jnp.where(row16 // 2 == i, bins_ref[index].astype(jnp.float32), values)
            turn = values * offset + quarter
            turn = turn - jnp.floor(turn + 0.5)
            rows = pl.ds(pl.multiple_of(r * 16, 16), 16)
            table[rows, :] = (weight * horner(turn * turn, COS_FIT)).astype(table.dtype)
            return 0

        lax.fori_loop(0, freq_rows // 16, table_rows, 0)

    table_chunk(0)
    whole = blocks.at[0 : snaps * ch_dev, :]
    pltpu.make_async_copy(whole, whole, load_sem).wait()

    def part(d):
        return pl.ds(pl.multiple_of(d * chunk_rows, chunk_rows), chunk_rows)

    def partner(j):
        if devices & (devices - 1):
            return lax.rem(me + j, devices)
        other = me
        for b in range(devices.bit_length() - 1):
            flip = 1 - 2 * lax.rem(lax.div(me, 2**b), 2)
            other = other + lax.rem(lax.div(j, 2**b), 2) * flip * 2**b
        return other

    def send_chunk(k, _):
        def transform(i, _):
            @pl.when(jnp.logical_and(k == 0, i == tiles // 2 - 1))
            def _():
                halo.wait()
                tail = blocks[snaps * ch_dev :, :]
                last = my_tm == tm_count - 1
                blocks[snaps * ch_dev :, :] = jnp.where(last, jnp.zeros_like(tail), tail)

            start = pl.multiple_of(i * 2 * LANES, 2 * LANES)
            here = blocks[pl.ds(start, 2 * LANES), :]
            after = blocks[pl.ds(start + ch_dev, 2 * LANES), :]
            out = product(table[:, :hop], here) + product(table[:, hop:], after)
            for j in range(2):
                rows = pl.ds(2 * i + j, freq_rows, stride=tiles)
                stage[rows, :] = out[:, j * LANES : (j + 1) * LANES]
            return 0

        lax.fori_loop(0, tiles // 2, transform, 0)

        def pack(d, _):
            send[k, part(d), :] = stage[part(d), :].astype(send.dtype)
            return 0

        lax.fori_loop(0, devices, pack, 0)

        def send_one(j, _):
            other = partner(devices - j)
            pltpu.make_async_remote_copy(
                src_ref=send.at[k, part(other), :],
                dst_ref=recv.at[k, me],
                send_sem=send_sems.at[k],
                recv_sem=recv_sems.at[k],
                device_id=(lax.div(other, tm_count), lax.rem(other, tm_count)),
                device_id_type=mesh_id,
            ).start()
            return 0

        lax.fori_loop(1, devices, send_one, 0)
        recv[k, me] = send[k, part(me), :]

        @pl.when(k + 1 < chunks)
        def _():
            table_chunk(k + 1)

        return 0

    lax.fori_loop(0, chunks, send_chunk, 0)

    point, spot = grid_place(slow_ref[...])
    place[...] = point
    for first in range(0, SET, 16):
        row = lax.broadcasted_iota(jnp.int32, (16, 1), 0) + first
        onehot[first : first + 16, :] = (row == spot).astype(jnp.float32).astype(onehot.dtype)
    sets[...] = jnp.zeros_like(sets)
    power[...] = jnp.zeros_like(power)

    others = all_digits.at[0 : chan_count - 1]
    pltpu.make_async_copy(others, others, digit_sems.at[1]).wait()
    pltpu.make_async_copy(others, others, digit_sems.at[0]).wait()
    for m in range(chan_count // 2):
        left = all_digits[2 * m].astype(jnp.float32)
        right = pltpu.roll(all_digits[2 * m + 1].astype(jnp.float32), half, 1)
        both = jnp.where(lane < half, left, right)
        for axis in range(2):
            high, low = both[2 * axis : 2 * axis + 1], both[2 * axis + 1 : 2 * axis + 2]
            positions[axis : axis + 1, m * LANES : (m + 1) * LANES] = 32.0 * high + low

    modulus = 5 * W // 2
    inner_step = lax.broadcasted_iota(jnp.int32, (8, 1), 0)
    inner_step = jnp.where(inner_step <= INNER, inner_step, SPAN).astype(jnp.float32)
    step = (lax.broadcasted_iota(jnp.int32, (REACH, 1), 0) + 1).astype(jnp.float32)

    def one_bin(k, local, _):
        f = k * per_chunk + local
        bin_value = bins_ref[me * per_dev + f].astype(jnp.float32)
        for axis, steps, cos_ref, sin_ref in ((0, inner_step, c0, s0), (1, step, c1, s1)):
            turn = positions[axis : axis + 1, :] * bin_value
            turn = (turn - modulus * jnp.floor(turn * (1.0 / modulus))) * (1.0 / modulus)
            turn = turn - jnp.floor(turn + 0.5)
            cosine, sine = circle(turn * steps)
            cos_ref[...] = cosine
            sin_ref[...] = sine
        for m in range(chan_count // 2):
            cols = slice(m * LANES, (m + 1) * LANES)
            cos_1, sin_1 = c0[INNER + 1 : INNER + 2, cols], s0[INNER + 1 : INNER + 2, cols]
            spins = [(cos_1, sin_1), (2.0 * cos_1 * cos_1 - 1.0, 2.0 * sin_1 * cos_1)]
            for t in range(tm_count):
                pairs = []
                for p in range(2):
                    rows = pl.ds(pl.multiple_of((2 * local + p) * tiles, tiles), tiles)
                    left = recv[k, 2 * m * tm_count + t, rows, :].astype(jnp.float32)
                    right = recv[k, (2 * m + 1) * tm_count + t, rows, :].astype(jnp.float32)
                    even = jnp.where(lane < half, left, pltpu.roll(right, half, 1))
                    odd = jnp.where(lane < half, pltpu.roll(left, half, 1), right)
                    pairs.append((even, odd))
                for parity in range(2):
                    re, im = pairs[0][parity], pairs[1][parity]
                    turned = [None] * TURNS
                    turned[OUTER] = (re, im)
                    for h, (cosine, sine) in enumerate(spins, 1):
                        cr, si, ci, sr = cosine * re, sine * im, cosine * im, sine * re
                        turned[OUTER + h] = (cr + si, ci - sr)
                        turned[OUTER - h] = (cr - si, ci + sr)
                    for h, (real, imag) in enumerate(turned):
                        top = 2 * side * h + (t * 2 + parity) * tiles
                        low = top + side
                        yt[top : top + tiles, cols] = real.astype(yt.dtype)
                        yt[low : low + tiles, cols] = imag.astype(yt.dtype)
                        yj[top : top + tiles, cols] = imag.astype(yj.dtype)
                        yj[low : low + tiles, cols] = (-real).astype(yj.dtype)

        cosines, sines = c1[...], s1[...]
        for l in range(INNER):
            cos_row, sin_row = c0[l + 1 : l + 2, :], s0[l + 1 : l + 2, :]
            rows = slice(l * REACH, (l + 1) * REACH)
            sets[0, rows, :] = (cos_row * cosines).astype(sets.dtype)
            sets[1, rows, :] = (sin_row * sines).astype(sets.dtype)
            sets[2, rows, :] = (sin_row * cosines).astype(sets.dtype)
            sets[3, rows, :] = (cos_row * sines).astype(sets.dtype)
        sets[0, SECOND:FIRST, :] = cosines.astype(sets.dtype)
        sets[3, SECOND:FIRST, :] = sines.astype(sets.dtype)
        flat = slice(FIRST, FIRST + 16)
        sets[0, flat, :] = jnp.concatenate([c0[...]] * 2, axis=0).astype(sets.dtype)
        sets[2, flat, :] = jnp.concatenate([s0[...]] * 2, axis=0).astype(sets.dtype)
        for q in range(4):
            dots[q] = product((yt if q < 2 else yj)[...], sets[q])
        for h in range(TURNS):
            rows = slice(2 * side * h, 2 * side * (h + 1))
            cc, ss, sc, cs = dots[0, rows, :], dots[1, rows, :], dots[2, rows, :], dots[3, rows, :]
            even_same, even_other = cc - ss, cc + ss
            odd_same, odd_other = sc + cs, sc - cs
            for q, value in enumerate(
                (even_same + odd_same, even_same - odd_same, even_other + odd_other, even_other - odd_other)
            ):
                total = jnp.sum(value * value, axis=0, keepdims=True)
                power[pl.ds(f * POINTS + 4 * h + q, 1), :] = total * scale
        return 0

    def one_chunk(k, _):
        arrived = recv.at[k, 0 : devices - 1]
        pltpu.make_async_copy(arrived, arrived, recv_sems.at[k]).wait()
        lax.fori_loop(0, per_chunk, functools.partial(one_bin, k), 0)
        return 0

    lax.fori_loop(0, chunks, one_chunk, 0)

    high = power[...].astype(jnp.bfloat16)
    rest = (power[...] - high.astype(jnp.float32)).astype(jnp.bfloat16)
    point_row = lax.broadcasted_iota(jnp.int32, (POINTS, 1), 0)
    own = mine.shape[2]
    for t in range(tm_count):
        cols = slice(t * own, (t + 1) * own)
        spread = jnp.dot(high, onehot[:, cols], preferred_element_type=jnp.float32)
        spread += jnp.dot(rest, onehot[:, cols], preferred_element_type=jnp.float32)
        here = point_row == place[:, cols]
        for f in range(per_dev):
            rows = spread[f * POINTS : (f + 1) * POINTS]
            mine[t, f : f + 1, :] = jnp.sum(jnp.where(here, rows, 0.0), axis=0, keepdims=True)
    exchanges = []
    for j in range(1, tm_count):
        other = lax.rem(my_tm + j, tm_count)
        copy = pltpu.make_async_remote_copy(
            src_ref=mine.at[other],
            dst_ref=swapped.at[my_tm],
            send_sem=power_sems.at[0, j - 1],
            recv_sem=power_sems.at[1, j - 1],
            device_id=(my_chan, other),
            device_id_type=mesh_id,
        )
        copy.start()
        exchanges.append(copy)
    swapped[my_tm] = mine[my_tm]
    for copy in exchanges:
        copy.wait()
    out_ref[...] = swapped[...]

    def drain(k, _):
        sent = send.at[k, 0 : (devices - 1) * chunk_rows, :]
        pltpu.make_async_copy(sent, sent, send_sems.at[k]).wait()
        return 0

    lax.fori_loop(0, chunks, drain, 0)


def shards(records, coords, bins, slow_index):
    ch_dev, local_samples = records.shape
    hop = W // 2
    snaps = local_samples // hop
    chan_count = lax.axis_size("chan")
    tm_count = lax.axis_size("tm")
    devices = chan_count * tm_count
    channels = ch_dev * chan_count
    freq = bins.shape[0]
    per_dev = freq // devices
    chunks = math.gcd(per_dev, CHUNKS)
    tiles = snaps * ch_dev // LANES
    chunk_rows = 2 * per_dev * tiles // chunks
    columns = TURNS * 4 * tm_count * tiles
    kept = 8 * ((per_dev + 7) // 8)
    own = slow_index.shape[1] // tm_count
    scale = 1.0 / (channels * snaps * tm_count)
    vmem = pl.BlockSpec(memory_space=pltpu.VMEM)
    smem = pl.BlockSpec(memory_space=pltpu.SMEM)
    inner_angles = pltpu.VMEM((8, channels), jnp.float32)
    angles = pltpu.VMEM((REACH, channels), jnp.float32)
    power = pl.pallas_call(
        functools.partial(kernel, scale, tm_count, chan_count),
        out_shape=jax.ShapeDtypeStruct((tm_count, kept, own), jnp.float32),
        in_specs=[smem, vmem, vmem, pl.BlockSpec(memory_space=pl.ANY)],
        out_specs=vmem,
        scratch_shapes=[
            pltpu.VMEM(((snaps + 1) * ch_dev, hop), jnp.bfloat16),
            pltpu.VMEM((2 * freq // chunks, W), jnp.bfloat16),
            pltpu.VMEM((2 * freq * tiles // chunks, LANES), jnp.float32),
            pltpu.VMEM((chunks, devices * chunk_rows, LANES), jnp.bfloat16),
            pltpu.VMEM((chunks, devices, chunk_rows, LANES), jnp.bfloat16),
            pltpu.VMEM((16, LANES), jnp.bfloat16),
            pltpu.VMEM((chan_count, 16, LANES), jnp.bfloat16),
            pltpu.VMEM((2, channels), jnp.float32),
            pltpu.VMEM((columns, channels), jnp.bfloat16),
            pltpu.VMEM((columns, channels), jnp.bfloat16),
            inner_angles, inner_angles, angles, angles,
            pltpu.VMEM((4, SET, channels), jnp.bfloat16),
            pltpu.VMEM((4, columns, SET), jnp.float32),
            pltpu.VMEM((per_dev * POINTS, SET), jnp.float32),
            pltpu.VMEM((1, slow_index.shape[1]), jnp.int32),
            pltpu.VMEM((SET, slow_index.shape[1]), jnp.bfloat16),
            pltpu.VMEM((tm_count, kept, own), jnp.float32),
            pltpu.VMEM((tm_count, kept, own), jnp.float32),
            pltpu.SemaphoreType.DMA,
            pltpu.SemaphoreType.DMA((2,)),
            pltpu.SemaphoreType.DMA((2,)),
            pltpu.SemaphoreType.DMA((chunks,)),
            pltpu.SemaphoreType.DMA((chunks,)),
            pltpu.SemaphoreType.DMA((2, tm_count)),
        ],
        compiler_params=pltpu.CompilerParams(
            collective_id=0, has_side_effects=True, vmem_limit_bytes=52 * 2**20
        ),
        cost_estimate=pl.CostEstimate(
            flops=8 * SET * columns * channels * per_dev,
            bytes_accessed=records.size * 2,
            transcendentals=0,
        ),
    )(bins, slow_index, coords, records)
    return power[:, :per_dev, :].reshape(tm_count * per_dev, own).T


def solution(mesh):
    return jax.shard_map(
        shards,
        mesh=mesh,
        in_specs=(P("chan", "tm"), P(None, "chan"), P(), P()),
        out_specs=P("tm", "chan"),
        check_vma=False,
    )
```

```python
import functools
import math

import jax
import jax.numpy as jnp
import numpy as np
from jax import lax
from jax.experimental import pallas as pl
from jax.experimental.pallas import tpu as pltpu
from jax.sharding import PartitionSpec as P

W = 2048
REACH = 32
LANES = 128
INNER = 6
OUTER = 2
SPAN = 2 * INNER + 1
TURNS = 2 * OUTER + 1
CHUNKS = 8


def circle_fit():
    u = 0.125 * (1.0 - np.cos(math.pi * (np.arange(400) + 0.5) / 400))
    t = np.sqrt(u)
    powers = u[:, None] ** np.arange(6)[None, :]
    scaled = powers * (4.0 ** np.arange(6))
    cos_fit = np.linalg.lstsq(scaled, np.cos(2 * math.pi * t), rcond=None)[0]
    sin_fit = np.linalg.lstsq(scaled, np.sin(2 * math.pi * t) / t, rcond=None)[0]
    back = 4.0 ** np.arange(6)
    return [float(v) for v in cos_fit * back], [float(v) for v in sin_fit * back]


COS_FIT, SIN_FIT = circle_fit()


def horner(u, fit):
    total = jnp.full_like(u, fit[-1])
    for value in fit[-2::-1]:
        total = total * u + value
    return total


def circle(t):
    t = t - jnp.floor(t + 0.5)
    u = t * t
    return horner(u, COS_FIT), t * horner(u, SIN_FIT)


SECOND = INNER * REACH
FIRST = SECOND + REACH
SET = 2 * LANES
POINTS = 8 * ((4 * TURNS + 7) // 8)


def grid_place(slow_index):
    first, second = slow_index[0:1, :], slow_index[1:2, :]
    turn = sum((first + REACH >= SPAN * h).astype(jnp.int32) for h in range(1, TURNS))
    inner = first - SPAN * (turn - OUTER)
    low0, low1 = (inner < 0).astype(jnp.int32), (second < 0).astype(jnp.int32)
    a0, a1 = jnp.abs(inner), jnp.abs(second)
    quad = jnp.where(low0 == low1, low0, 2 + low0)
    quad = jnp.where(a0 == 0, low1, jnp.where(a1 == 0, low0, quad))
    lane = jnp.where(a0 == 0, SECOND + a1 - 1, (a0 - 1) * REACH + a1 - 1)
    return turn * 4 + quad, jnp.where(a1 == 0, FIRST + a0, lane)


def product(rows, columns):
    return lax.dot_general(
        rows, columns, (((1,), (1,)), ((), ())), preferred_element_type=jnp.float32
    )


def kernel(
    scale, tm_count, chan_count, bins_in, slow_in, coords_in, records_ref, out_ref,
    bins_ref, slow_ref, coords_ref,
    blocks, table, stage, send, recv, digits, all_digits, positions,
    yt, yj, c0, s0, c1, s1, sets, dots, power, place, onehot, mine, swapped,
    load_sem, small_sems, halo_sems, digit_sems, send_sems, recv_sems, power_sems,
):
    devices = tm_count * chan_count
    chunks, _, chunk_rows, _ = recv.shape
    ch_dev, local_samples = records_ref.shape
    hop = W // 2
    snaps = local_samples // hop
    tiles = snaps * ch_dev // LANES
    per_dev = bins_ref.shape[0] // devices
    per_chunk = per_dev // chunks
    freq_rows = table.shape[0]
    half = LANES // 2
    side = tm_count * 2 * tiles
    my_chan, my_tm = lax.axis_index("chan"), lax.axis_index("tm")
    me = my_chan * tm_count + my_tm
    lane = lax.broadcasted_iota(jnp.int32, (1, LANES), 1)
    mesh_id = pl.DeviceIdType.MESH

    barrier = pltpu.get_barrier_semaphore()

    def greet(j, _):
        other = lax.rem(me + j, devices)
        pl.semaphore_signal(
            barrier,
            inc=1,
            device_id=(lax.div(other, tm_count), lax.rem(other, tm_count)),
            device_id_type=mesh_id,
        )
        return 0

    lax.fori_loop(1, devices, greet, 0)

    small = [
        pltpu.make_async_copy(source, target, small_sems.at[i])
        for i, (source, target) in enumerate(
            ((coords_in, coords_ref), (bins_in, bins_ref), (slow_in, slow_ref))
        )
    ]
    for copy in small:
        copy.start()

    def load(n, _):
        pltpu.make_async_copy(
            records_ref.at[:, pl.ds(pl.multiple_of(n * hop, hop), hop)],
            blocks.at[pl.ds(pl.multiple_of(n * ch_dev, ch_dev), ch_dev), :],
            load_sem,
        ).start()
        return 0

    lax.fori_loop(0, snaps, load, 0)
    digits[...] = jnp.zeros_like(digits)
    for copy in small:
        copy.wait()
    for axis in range(2):
        values = coords_ref[axis : axis + 1, :].astype(jnp.float32)
        high = jnp.floor(values * (1.0 / 32.0))
        digits[2 * axis : 2 * axis + 1, 0:ch_dev] = high.astype(digits.dtype)
        digits[2 * axis + 1 : 2 * axis + 2, 0:ch_dev] = (values - 32.0 * high).astype(digits.dtype)
    all_digits[my_chan] = digits[...]
    pl.semaphore_wait(barrier, devices - 1)

    halo = pltpu.make_async_remote_copy(
        src_ref=records_ref.at[:, 0:hop],
        dst_ref=blocks.at[snaps * ch_dev : (snaps + 1) * ch_dev, :],
        send_sem=halo_sems.at[0],
        recv_sem=halo_sems.at[1],
        device_id=(my_chan, lax.rem(my_tm + tm_count - 1, tm_count)),
        device_id_type=mesh_id,
    )
    halo.start()

    def tell(j, _):
        pltpu.make_async_remote_copy(
            src_ref=digits,
            dst_ref=all_digits.at[my_chan],
            send_sem=digit_sems.at[0],
            recv_sem=digit_sems.at[1],
            device_id=(lax.rem(my_chan + j, chan_count), my_tm),
            device_id_type=mesh_id,
        ).start()
        return 0

    lax.fori_loop(1, chan_count, tell, 0)

    offset = lax.broadcasted_iota(jnp.int32, (1, W), 1).astype(jnp.float32) * (1.0 / W)
    weight = (0.5 - 0.5 * circle(offset)[0]) * math.sqrt(8.0 / (3.0 * W))
    row16 = lax.broadcasted_iota(jnp.int32, (16, 1), 0)
    quarter = lax.rem(row16, 2).astype(jnp.float32) * 0.25

    def table_chunk(k):
        def table_rows(r, _):
            values = jnp.zeros((16, 1), jnp.float32)
            for i in range(8):
                b = r * 8 + i
                index = lax.div(b, per_chunk) * per_dev + k * per_chunk + lax.rem(b, per_chunk)
                values = jnp.where(row16 // 2 == i, bins_ref[index].astype(jnp.float32), values)
            turn = values * offset + quarter
            turn = turn - jnp.floor(turn + 0.5)
            rows = pl.ds(pl.multiple_of(r * 16, 16), 16)
            table[rows, :] = (weight * horner(turn * turn, COS_FIT)).astype(table.dtype)
            return 0

        lax.fori_loop(0, freq_rows // 16, table_rows, 0)

    table_chunk(0)
    whole = blocks.at[0 : snaps * ch_dev, :]
    pltpu.make_async_copy(whole, whole, load_sem).wait()

    def part(d):
        return pl.ds(pl.multiple_of(d * chunk_rows, chunk_rows), chunk_rows)

    def partner(j):
        if devices & (devices - 1):
            return lax.rem(me + j, devices)
        other = me
        for b in range(devices.bit_length() - 1):
            flip = 1 - 2 * lax.rem(lax.div(me, 2**b), 2)
            other = other + lax.rem(lax.div(j, 2**b), 2) * flip * 2**b
        return other

    def send_chunk(k, _):
        def transform(i, _):
            @pl.when(jnp.logical_and(k == 0, i == tiles // 2 - 1))
            def _():
                halo.wait()
                tail = blocks[snaps * ch_dev :, :]
                last = my_tm == tm_count - 1
                blocks[snaps * ch_dev :, :] = jnp.where(last, jnp.zeros_like(tail), tail)

            start = pl.multiple_of(i * 2 * LANES, 2 * LANES)
            here = blocks[pl.ds(start, 2 * LANES), :]
            after = blocks[pl.ds(start + ch_dev, 2 * LANES), :]
            out = product(table[:, :hop], here) + product(table[:, hop:], after)
            for j in range(2):
                rows = pl.ds(2 * i + j, freq_rows, stride=tiles)
                stage[rows, :] = out[:, j * LANES : (j + 1) * LANES]
            return 0

        lax.fori_loop(0, tiles // 2, transform, 0)

        def pack(d, _):
            send[k, part(d), :] = stage[part(d), :].astype(send.dtype)
            return 0

        lax.fori_loop(0, devices, pack, 0)

        def send_one(j, _):
            other = partner(devices - j)
            pltpu.make_async_remote_copy(
                src_ref=send.at[k, part(other), :],
                dst_ref=recv.at[k, me],
                send_sem=send_sems.at[k],
                recv_sem=recv_sems.at[k],
                device_id=(lax.div(other, tm_count), lax.rem(other, tm_count)),
                device_id_type=mesh_id,
            ).start()
            return 0

        lax.fori_loop(1, devices, send_one, 0)
        recv[k, me] = send[k, part(me), :]

        @pl.when(k + 1 < chunks)
        def _():
            table_chunk(k + 1)

        return 0

    lax.fori_loop(0, chunks, send_chunk, 0)

    point, spot = grid_place(slow_ref[...])
    place[...] = point
    for first in range(0, SET, 16):
        row = lax.broadcasted_iota(jnp.int32, (16, 1), 0) + first
        onehot[first : first + 16, :] = (row == spot).astype(jnp.float32).astype(onehot.dtype)
    sets[...] = jnp.zeros_like(sets)
    power[...] = jnp.zeros_like(power)

    others = all_digits.at[0 : chan_count - 1]
    pltpu.make_async_copy(others, others, digit_sems.at[1]).wait()
    pltpu.make_async_copy(others, others, digit_sems.at[0]).wait()
    for m in range(chan_count // 2):
        left = all_digits[2 * m].astype(jnp.float32)
        right = pltpu.roll(all_digits[2 * m + 1].astype(jnp.float32), half, 1)
        both = jnp.where(lane < half, left, right)
        for axis in range(2):
            high, low = both[2 * axis : 2 * axis + 1], both[2 * axis + 1 : 2 * axis + 2]
            positions[axis : axis + 1, m * LANES : (m + 1) * LANES] = 32.0 * high + low

    modulus = 5 * W // 2
    inner_step = lax.broadcasted_iota(jnp.int32, (8, 1), 0)
    inner_step = jnp.where(inner_step <= INNER, inner_step, SPAN).astype(jnp.float32)
    step = (lax.broadcasted_iota(jnp.int32, (REACH, 1), 0) + 1).astype(jnp.float32)

    def one_bin(k, local, _):
        f = k * per_chunk + local
        bin_value = bins_ref[me * per_dev + f].astype(jnp.float32)
        for axis, steps, cos_ref, sin_ref in ((0, inner_step, c0, s0), (1, step, c1, s1)):
            turn = positions[axis : axis + 1, :] * bin_value
            turn = (turn - modulus * jnp.floor(turn * (1.0 / modulus))) * (1.0 / modulus)
            turn = turn - jnp.floor(turn + 0.5)
            cosine, sine = circle(turn * steps)
            cos_ref[...] = cosine
            sin_ref[...] = sine
        for m in range(chan_count // 2):
            cols = slice(m * LANES, (m + 1) * LANES)
            cos_1, sin_1 = c0[INNER + 1 : INNER + 2, cols], s0[INNER + 1 : INNER + 2, cols]
            spins = [(cos_1, sin_1), (2.0 * cos_1 * cos_1 - 1.0, 2.0 * sin_1 * cos_1)]
            for t in range(tm_count):
                pairs = []
                for p in range(2):
                    rows = pl.ds(pl.multiple_of((2 * local + p) * tiles, tiles), tiles)
                    left = recv[k, 2 * m * tm_count + t, rows, :].astype(jnp.float32)
                    right = recv[k, (2 * m + 1) * tm_count + t, rows, :].astype(jnp.float32)
                    even = jnp.where(lane < half, left, pltpu.roll(right, half, 1))
                    odd = jnp.where(lane < half, pltpu.roll(left, half, 1), right)
                    pairs.append((even, odd))
                for parity in range(2):
                    re, im = pairs[0][parity], pairs[1][parity]
                    turned = [None] * TURNS
                    turned[OUTER] = (re, im)
                    for h, (cosine, sine) in enumerate(spins, 1):
                        cr, si, ci, sr = cosine * re, sine * im, cosine * im, sine * re
                        turned[OUTER + h] = (cr + si, ci - sr)
                        turned[OUTER - h] = (cr - si, ci + sr)
                    for h, (real, imag) in enumerate(turned):
                        top = 2 * side * h + (t * 2 + parity) * tiles
                        low = top + side
                        yt[top : top + tiles, cols] = real.astype(yt.dtype)
                        yt[low : low + tiles, cols] = imag.astype(yt.dtype)
                        yj[top : top + tiles, cols] = imag.astype(yj.dtype)
                        yj[low : low + tiles, cols] = (-real).astype(yj.dtype)

        cosines, sines = c1[...], s1[...]
        for l in range(INNER):
            cos_row, sin_row = c0[l + 1 : l + 2, :], s0[l + 1 : l + 2, :]
            rows = slice(l * REACH, (l + 1) * REACH)
            sets[0, rows, :] = (cos_row * cosines).astype(sets.dtype)
            sets[1, rows, :] = (sin_row * sines).astype(sets.dtype)
            sets[2, rows, :] = (sin_row * cosines).astype(sets.dtype)
            sets[3, rows, :] = (cos_row * sines).astype(sets.dtype)
        sets[0, SECOND:FIRST, :] = cosines.astype(sets.dtype)
        sets[3, SECOND:FIRST, :] = sines.astype(sets.dtype)
        flat = slice(FIRST, FIRST + 16)
        sets[0, flat, :] = jnp.concatenate([c0[...]] * 2, axis=0).astype(sets.dtype)
        sets[2, flat, :] = jnp.concatenate([s0[...]] * 2, axis=0).astype(sets.dtype)
        for q in range(4):
            dots[q] = product((yt if q < 2 else yj)[...], sets[q])
        for h in range(TURNS):
            rows = slice(2 * side * h, 2 * side * (h + 1))
            cc, ss, sc, cs = dots[0, rows, :], dots[1, rows, :], dots[2, rows, :], dots[3, rows, :]
            even_same, even_other = cc - ss, cc + ss
            odd_same, odd_other = sc + cs, sc - cs
            for q, value in enumerate(
                (even_same + odd_same, even_same - odd_same, even_other + odd_other, even_other - odd_other)
            ):
                total = jnp.sum(value * value, axis=0, keepdims=True)
                power[pl.ds(f * POINTS + 4 * h + q, 1), :] = total * scale
        return 0

    def one_chunk(k, _):
        arrived = recv.at[k, 0 : devices - 1]
        pltpu.make_async_copy(arrived, arrived, recv_sems.at[k]).wait()
        lax.fori_loop(0, per_chunk, functools.partial(one_bin, k), 0)
        return 0

    lax.fori_loop(0, chunks, one_chunk, 0)

    high = power[...].astype(jnp.bfloat16)
    rest = (power[...] - high.astype(jnp.float32)).astype(jnp.bfloat16)
    point_row = lax.broadcasted_iota(jnp.int32, (POINTS, 1), 0)
    own = mine.shape[2]
    for t in range(tm_count):
        cols = slice(t * own, (t + 1) * own)
        spread = jnp.dot(high, onehot[:, cols], preferred_element_type=jnp.float32)
        spread += jnp.dot(rest, onehot[:, cols], preferred_element_type=jnp.float32)
        here = point_row == place[:, cols]
        for f in range(per_dev):
            rows = spread[f * POINTS : (f + 1) * POINTS]
            mine[t, f : f + 1, :] = jnp.sum(jnp.where(here, rows, 0.0), axis=0, keepdims=True)
    exchanges = []
    for j in range(1, tm_count):
        other = lax.rem(my_tm + j, tm_count)
        copy = pltpu.make_async_remote_copy(
            src_ref=mine.at[other],
            dst_ref=swapped.at[my_tm],
            send_sem=power_sems.at[0, j - 1],
            recv_sem=power_sems.at[1, j - 1],
            device_id=(my_chan, other),
            device_id_type=mesh_id,
        )
        copy.start()
        exchanges.append(copy)
    swapped[my_tm] = mine[my_tm]
    for copy in exchanges:
        copy.wait()
    out_ref[...] = swapped[...]

    def drain(k, _):
        sent = send.at[k, 0 : (devices - 1) * chunk_rows, :]
        pltpu.make_async_copy(sent, sent, send_sems.at[k]).wait()
        return 0

    lax.fori_loop(0, chunks, drain, 0)


def shards(records, coords, bins, slow_index):
    ch_dev, local_samples = records.shape
    hop = W // 2
    snaps = local_samples // hop
    chan_count = lax.axis_size("chan")
    tm_count = lax.axis_size("tm")
    devices = chan_count * tm_count
    channels = ch_dev * chan_count
    freq = bins.shape[0]
    per_dev = freq // devices
    chunks = math.gcd(per_dev, CHUNKS)
    tiles = snaps * ch_dev // LANES
    chunk_rows = 2 * per_dev * tiles // chunks
    columns = TURNS * 4 * tm_count * tiles
    kept = 8 * ((per_dev + 7) // 8)
    own = slow_index.shape[1] // tm_count
    scale = 1.0 / (channels * snaps * tm_count)
    vmem = pl.BlockSpec(memory_space=pltpu.VMEM)
    inner_angles = pltpu.VMEM((8, channels), jnp.float32)
    angles = pltpu.VMEM((REACH, channels), jnp.float32)
    power = pl.pallas_call(
        functools.partial(kernel, scale, tm_count, chan_count),
        out_shape=jax.ShapeDtypeStruct((tm_count, kept, own), jnp.float32),
        in_specs=[pl.BlockSpec(memory_space=pl.ANY)] * 4,
        out_specs=vmem,
        scratch_shapes=[
            pltpu.SMEM(bins.shape, jnp.int32),
            pltpu.VMEM(slow_index.shape, jnp.int32),
            pltpu.VMEM(coords.shape, jnp.int32),
            pltpu.VMEM(((snaps + 1) * ch_dev, hop), jnp.bfloat16),
            pltpu.VMEM((2 * freq // chunks, W), jnp.bfloat16),
            pltpu.VMEM((2 * freq * tiles // chunks, LANES), jnp.float32),
            pltpu.VMEM((chunks, devices * chunk_rows, LANES), jnp.bfloat16),
            pltpu.VMEM((chunks, devices, chunk_rows, LANES), jnp.bfloat16),
            pltpu.VMEM((16, LANES), jnp.bfloat16),
            pltpu.VMEM((chan_count, 16, LANES), jnp.bfloat16),
            pltpu.VMEM((2, channels), jnp.float32),
            pltpu.VMEM((columns, channels), jnp.bfloat16),
            pltpu.VMEM((columns, channels), jnp.bfloat16),
            inner_angles, inner_angles, angles, angles,
            pltpu.VMEM((4, SET, channels), jnp.bfloat16),
            pltpu.VMEM((4, columns, SET), jnp.float32),
            pltpu.VMEM((per_dev * POINTS, SET), jnp.float32),
            pltpu.VMEM((1, slow_index.shape[1]), jnp.int32),
            pltpu.VMEM((SET, slow_index.shape[1]), jnp.bfloat16),
            pltpu.VMEM((tm_count, kept, own), jnp.float32),
            pltpu.VMEM((tm_count, kept, own), jnp.float32),
            pltpu.SemaphoreType.DMA,
            pltpu.SemaphoreType.DMA((3,)),
            pltpu.SemaphoreType.DMA((2,)),
            pltpu.SemaphoreType.DMA((2,)),
            pltpu.SemaphoreType.DMA((chunks,)),
            pltpu.SemaphoreType.DMA((chunks,)),
            pltpu.SemaphoreType.DMA((2, tm_count)),
        ],
        compiler_params=pltpu.CompilerParams(
            collective_id=0, has_side_effects=True, vmem_limit_bytes=52 * 2**20
        ),
        cost_estimate=pl.CostEstimate(
            flops=8 * SET * columns * channels * per_dev,
            bytes_accessed=records.size * 2,
            transcendentals=0,
        ),
    )(bins, slow_index, coords, records)
    return power[:, :per_dev, :].reshape(tm_count * per_dev, own).T


def solution(mesh):
    return jax.shard_map(
        shards,
        mesh=mesh,
        in_specs=(P("chan", "tm"), P(None, "chan"), P(), P()),
        out_specs=P("tm", "chan"),
        check_vma=False,
    )
```

```python
import functools
import math

import jax
import jax.numpy as jnp
import numpy as np
from jax import lax
from jax.experimental import pallas as pl
from jax.experimental.pallas import tpu as pltpu
from jax.sharding import PartitionSpec as P

W = 2048
REACH = 32
LANES = 128
INNER = 6
OUTER = 2
SPAN = 2 * INNER + 1
TURNS = 2 * OUTER + 1
CHUNKS = 4


def circle_fit():
    u = 0.125 * (1.0 - np.cos(math.pi * (np.arange(400) + 0.5) / 400))
    t = np.sqrt(u)
    powers = u[:, None] ** np.arange(6)[None, :]
    scaled = powers * (4.0 ** np.arange(6))
    cos_fit = np.linalg.lstsq(scaled, np.cos(2 * math.pi * t), rcond=None)[0]
    sin_fit = np.linalg.lstsq(scaled, np.sin(2 * math.pi * t) / t, rcond=None)[0]
    back = 4.0 ** np.arange(6)
    return [float(v) for v in cos_fit * back], [float(v) for v in sin_fit * back]


COS_FIT, SIN_FIT = circle_fit()


def horner(u, fit):
    total = jnp.full_like(u, fit[-1])
    for value in fit[-2::-1]:
        total = total * u + value
    return total


def circle(t):
    t = t - jnp.floor(t + 0.5)
    u = t * t
    return horner(u, COS_FIT), t * horner(u, SIN_FIT)


SECOND = INNER * REACH
FIRST = SECOND + REACH
SET = 2 * LANES
POINTS = 8 * ((4 * TURNS + 7) // 8)


def grid_place(slow_index):
    first, second = slow_index[0:1, :], slow_index[1:2, :]
    turn = sum((first + REACH >= SPAN * h).astype(jnp.int32) for h in range(1, TURNS))
    inner = first - SPAN * (turn - OUTER)
    low0, low1 = (inner < 0).astype(jnp.int32), (second < 0).astype(jnp.int32)
    a0, a1 = jnp.abs(inner), jnp.abs(second)
    quad = jnp.where(low0 == low1, low0, 2 + low0)
    quad = jnp.where(a0 == 0, low1, jnp.where(a1 == 0, low0, quad))
    lane = jnp.where(a0 == 0, SECOND + a1 - 1, (a0 - 1) * REACH + a1 - 1)
    return turn * 4 + quad, jnp.where(a1 == 0, FIRST + a0, lane)


def product(rows, columns):
    return lax.dot_general(
        rows, columns, (((1,), (1,)), ((), ())), preferred_element_type=jnp.float32
    )


def kernel(
    scale, tm_count, chan_count, bins_in, slow_in, coords_in, records_ref, out_ref,
    bins_ref, slow_ref, coords_ref,
    blocks, table, stage, send, recv, digits, all_digits, positions,
    yt, yj, c0, s0, c1, s1, sets, dots, power, place, onehot, mine, swapped,
    load_sem, small_sems, halo_sems, digit_sems, send_sems, recv_sems, power_sems,
):
    devices = tm_count * chan_count
    chunks, _, chunk_rows, _ = recv.shape
    ch_dev, local_samples = records_ref.shape
    hop = W // 2
    snaps = local_samples // hop
    tiles = snaps * ch_dev // LANES
    per_dev = bins_ref.shape[0] // devices
    per_chunk = per_dev // chunks
    freq_rows = table.shape[0]
    half = LANES // 2
    side = tm_count * 2 * tiles
    my_chan, my_tm = lax.axis_index("chan"), lax.axis_index("tm")
    me = my_chan * tm_count + my_tm
    lane = lax.broadcasted_iota(jnp.int32, (1, LANES), 1)
    mesh_id = pl.DeviceIdType.MESH

    barrier = pltpu.get_barrier_semaphore()

    def greet(j, _):
        other = lax.rem(me + j, devices)
        pl.semaphore_signal(
            barrier,
            inc=1,
            device_id=(lax.div(other, tm_count), lax.rem(other, tm_count)),
            device_id_type=mesh_id,
        )
        return 0

    lax.fori_loop(1, devices, greet, 0)

    small = [
        pltpu.make_async_copy(source, target, small_sems.at[i])
        for i, (source, target) in enumerate(
            ((coords_in, coords_ref), (bins_in, bins_ref), (slow_in, slow_ref))
        )
    ]
    for copy in small:
        copy.start()

    def load(n, _):
        pltpu.make_async_copy(
            records_ref.at[:, pl.ds(pl.multiple_of(n * hop, hop), hop)],
            blocks.at[pl.ds(pl.multiple_of(n * ch_dev, ch_dev), ch_dev), :],
            load_sem,
        ).start()
        return 0

    lax.fori_loop(0, snaps, load, 0)
    digits[...] = jnp.zeros_like(digits)
    for copy in small:
        copy.wait()
    for axis in range(2):
        values = coords_ref[axis : axis + 1, :].astype(jnp.float32)
        high = jnp.floor(values * (1.0 / 32.0))
        digits[2 * axis : 2 * axis + 1, 0:ch_dev] = high.astype(digits.dtype)
        digits[2 * axis + 1 : 2 * axis + 2, 0:ch_dev] = (values - 32.0 * high).astype(digits.dtype)
    all_digits[my_chan] = digits[...]
    pl.semaphore_wait(barrier, devices - 1)

    halo = pltpu.make_async_remote_copy(
        src_ref=records_ref.at[:, 0:hop],
        dst_ref=blocks.at[snaps * ch_dev : (snaps + 1) * ch_dev, :],
        send_sem=halo_sems.at[0],
        recv_sem=halo_sems.at[1],
        device_id=(my_chan, lax.rem(my_tm + tm_count - 1, tm_count)),
        device_id_type=mesh_id,
    )
    halo.start()

    def tell(j, _):
        pltpu.make_async_remote_copy(
            src_ref=digits,
            dst_ref=all_digits.at[my_chan],
            send_sem=digit_sems.at[0],
            recv_sem=digit_sems.at[1],
            device_id=(lax.rem(my_chan + j, chan_count), my_tm),
            device_id_type=mesh_id,
        ).start()
        return 0

    lax.fori_loop(1, chan_count, tell, 0)

    offset = lax.broadcasted_iota(jnp.int32, (1, W), 1).astype(jnp.float32) * (1.0 / W)
    weight = (0.5 - 0.5 * circle(offset)[0]) * math.sqrt(8.0 / (3.0 * W))
    row16 = lax.broadcasted_iota(jnp.int32, (16, 1), 0)
    quarter = lax.rem(row16, 2).astype(jnp.float32) * 0.25

    def table_chunk(k):
        def table_rows(r, _):
            values = jnp.zeros((16, 1), jnp.float32)
            for i in range(8):
                b = r * 8 + i
                index = lax.div(b, per_chunk) * per_dev + k * per_chunk + lax.rem(b, per_chunk)
                values = jnp.where(row16 // 2 == i, bins_ref[index].astype(jnp.float32), values)
            turn = values * offset + quarter
            turn = turn - jnp.floor(turn + 0.5)
            rows = pl.ds(pl.multiple_of(r * 16, 16), 16)
            table[rows, :] = (weight * horner(turn * turn, COS_FIT)).astype(table.dtype)
            return 0

        lax.fori_loop(0, freq_rows // 16, table_rows, 0)

    table_chunk(0)
    whole = blocks.at[0 : snaps * ch_dev, :]
    pltpu.make_async_copy(whole, whole, load_sem).wait()

    def part(d):
        return pl.ds(pl.multiple_of(d * chunk_rows, chunk_rows), chunk_rows)

    def partner(j):
        if devices & (devices - 1):
            return lax.rem(me + j, devices)
        other = me
        for b in range(devices.bit_length() - 1):
            flip = 1 - 2 * lax.rem(lax.div(me, 2**b), 2)
            other = other + lax.rem(lax.div(j, 2**b), 2) * flip * 2**b
        return other

    def send_chunk(k, _):
        def transform(i, _):
            @pl.when(jnp.logical_and(k == 0, i == tiles // 2 - 1))
            def _():
                halo.wait()
                tail = blocks[snaps * ch_dev :, :]
                last = my_tm == tm_count - 1
                blocks[snaps * ch_dev :, :] = jnp.where(last, jnp.zeros_like(tail), tail)

            start = pl.multiple_of(i * 2 * LANES, 2 * LANES)
            here = blocks[pl.ds(start, 2 * LANES), :]
            after = blocks[pl.ds(start + ch_dev, 2 * LANES), :]
            out = product(table[:, :hop], here) + product(table[:, hop:], after)
            for j in range(2):
                rows = pl.ds(2 * i + j, freq_rows, stride=tiles)
                stage[rows, :] = out[:, j * LANES : (j + 1) * LANES]
            return 0

        lax.fori_loop(0, tiles // 2, transform, 0)

        def pack(d, _):
            send[k, part(d), :] = stage[part(d), :].astype(send.dtype)
            return 0

        lax.fori_loop(0, devices, pack, 0)

        def send_one(j, _):
            other = partner(j // 2 + lax.rem(j, 2) * (devices // 2))
            pltpu.make_async_remote_copy(
                src_ref=send.at[k, part(other), :],
                dst_ref=recv.at[k, me],
                send_sem=send_sems.at[k],
                recv_sem=recv_sems.at[k],
                device_id=(lax.div(other, tm_count), lax.rem(other, tm_count)),
                device_id_type=mesh_id,
            ).start()
            return 0

        lax.fori_loop(1, devices, send_one, 0)
        recv[k, me] = send[k, part(me), :]

        @pl.when(k + 1 < chunks)
        def _():
            table_chunk(k + 1)

        return 0

    lax.fori_loop(0, chunks, send_chunk, 0)

    point, spot = grid_place(slow_ref[...])
    place[...] = point
    for first in range(0, SET, 16):
        row = lax.broadcasted_iota(jnp.int32, (16, 1), 0) + first
        onehot[first : first + 16, :] = (row == spot).astype(jnp.float32).astype(onehot.dtype)
    sets[...] = jnp.zeros_like(sets)
    power[...] = jnp.zeros_like(power)

    others = all_digits.at[0 : chan_count - 1]
    pltpu.make_async_copy(others, others, digit_sems.at[1]).wait()
    pltpu.make_async_copy(others, others, digit_sems.at[0]).wait()
    for m in range(chan_count // 2):
        left = all_digits[2 * m].astype(jnp.float32)
        right = pltpu.roll(all_digits[2 * m + 1].astype(jnp.float32), half, 1)
        both = jnp.where(lane < half, left, right)
        for axis in range(2):
            high, low = both[2 * axis : 2 * axis + 1], both[2 * axis + 1 : 2 * axis + 2]
            positions[axis : axis + 1, m * LANES : (m + 1) * LANES] = 32.0 * high + low

    modulus = 5 * W // 2
    inner_step = lax.broadcasted_iota(jnp.int32, (8, 1), 0)
    inner_step = jnp.where(inner_step <= INNER, inner_step, SPAN).astype(jnp.float32)
    step = (lax.broadcasted_iota(jnp.int32, (REACH, 1), 0) + 1).astype(jnp.float32)

    def one_bin(k, local, _):
        f = k * per_chunk + local
        bin_value = bins_ref[me * per_dev + f].astype(jnp.float32)
        for axis, steps, cos_ref, sin_ref in ((0, inner_step, c0, s0), (1, step, c1, s1)):
            turn = positions[axis : axis + 1, :] * bin_value
            turn = (turn - modulus * jnp.floor(turn * (1.0 / modulus))) * (1.0 / modulus)
            turn = turn - jnp.floor(turn + 0.5)
            cosine, sine = circle(turn * steps)
            cos_ref[...] = cosine
            sin_ref[...] = sine
        for m in range(chan_count // 2):
            cols = slice(m * LANES, (m + 1) * LANES)
            cos_1, sin_1 = c0[INNER + 1 : INNER + 2, cols], s0[INNER + 1 : INNER + 2, cols]
            spins = [(cos_1, sin_1), (2.0 * cos_1 * cos_1 - 1.0, 2.0 * sin_1 * cos_1)]
            for t in range(tm_count):
                pairs = []
                for p in range(2):
                    rows = pl.ds(pl.multiple_of((2 * local + p) * tiles, tiles), tiles)
                    left = recv[k, 2 * m * tm_count + t, rows, :].astype(jnp.float32)
                    right = recv[k, (2 * m + 1) * tm_count + t, rows, :].astype(jnp.float32)
                    even = jnp.where(lane < half, left, pltpu.roll(right, half, 1))
                    odd = jnp.where(lane < half, pltpu.roll(left, half, 1), right)
                    pairs.append((even, odd))
                for parity in range(2):
                    re, im = pairs[0][parity], pairs[1][parity]
                    turned = [None] * TURNS
                    turned[OUTER] = (re, im)
                    for h, (cosine, sine) in enumerate(spins, 1):
                        cr, si, ci, sr = cosine * re, sine * im, cosine * im, sine * re
                        turned[OUTER + h] = (cr + si, ci - sr)
                        turned[OUTER - h] = (cr - si, ci + sr)
                    for h, (real, imag) in enumerate(turned):
                        top = 2 * side * h + (t * 2 + parity) * tiles
                        low = top + side
                        yt[top : top + tiles, cols] = real.astype(yt.dtype)
                        yt[low : low + tiles, cols] = imag.astype(yt.dtype)
                        yj[top : top + tiles, cols] = imag.astype(yj.dtype)
                        yj[low : low + tiles, cols] = (-real).astype(yj.dtype)

        cosines, sines = c1[...], s1[...]
        for l in range(INNER):
            cos_row, sin_row = c0[l + 1 : l + 2, :], s0[l + 1 : l + 2, :]
            rows = slice(l * REACH, (l + 1) * REACH)
            sets[0, rows, :] = (cos_row * cosines).astype(sets.dtype)
            sets[1, rows, :] = (sin_row * sines).astype(sets.dtype)
            sets[2, rows, :] = (sin_row * cosines).astype(sets.dtype)
            sets[3, rows, :] = (cos_row * sines).astype(sets.dtype)
        sets[0, SECOND:FIRST, :] = cosines.astype(sets.dtype)
        sets[3, SECOND:FIRST, :] = sines.astype(sets.dtype)
        flat = slice(FIRST, FIRST + 16)
        sets[0, flat, :] = jnp.concatenate([c0[...]] * 2, axis=0).astype(sets.dtype)
        sets[2, flat, :] = jnp.concatenate([s0[...]] * 2, axis=0).astype(sets.dtype)
        for q in range(4):
            dots[q] = product((yt if q < 2 else yj)[...], sets[q])
        for h in range(TURNS):
            rows = slice(2 * side * h, 2 * side * (h + 1))
            cc, ss, sc, cs = dots[0, rows, :], dots[1, rows, :], dots[2, rows, :], dots[3, rows, :]
            even_same, even_other = cc - ss, cc + ss
            odd_same, odd_other = sc + cs, sc - cs
            for q, value in enumerate(
                (even_same + odd_same, even_same - odd_same, even_other + odd_other, even_other - odd_other)
            ):
                total = jnp.sum(value * value, axis=0, keepdims=True)
                power[pl.ds(f * POINTS + 4 * h + q, 1), :] = total * scale
        return 0

    def one_chunk(k, _):
        arrived = recv.at[k, 0 : devices - 1]
        pltpu.make_async_copy(arrived, arrived, recv_sems.at[k]).wait()
        lax.fori_loop(0, per_chunk, functools.partial(one_bin, k), 0)
        return 0

    lax.fori_loop(0, chunks, one_chunk, 0)

    high = power[...].astype(jnp.bfloat16)
    rest = (power[...] - high.astype(jnp.float32)).astype(jnp.bfloat16)
    point_row = lax.broadcasted_iota(jnp.int32, (POINTS, 1), 0)
    own = mine.shape[2]
    for t in range(tm_count):
        cols = slice(t * own, (t + 1) * own)
        spread = jnp.dot(high, onehot[:, cols], preferred_element_type=jnp.float32)
        spread += jnp.dot(rest, onehot[:, cols], preferred_element_type=jnp.float32)
        here = point_row == place[:, cols]
        for f in range(per_dev):
            rows = spread[f * POINTS : (f + 1) * POINTS]
            mine[t, f : f + 1, :] = jnp.sum(jnp.where(here, rows, 0.0), axis=0, keepdims=True)
    exchanges = []
    for j in range(1, tm_count):
        other = lax.rem(my_tm + j, tm_count)
        copy = pltpu.make_async_remote_copy(
            src_ref=mine.at[other],
            dst_ref=swapped.at[my_tm],
            send_sem=power_sems.at[0, j - 1],
            recv_sem=power_sems.at[1, j - 1],
            device_id=(my_chan, other),
            device_id_type=mesh_id,
        )
        copy.start()
        exchanges.append(copy)
    swapped[my_tm] = mine[my_tm]
    for copy in exchanges:
        copy.wait()
    out_ref[...] = swapped[...]

    def drain(k, _):
        sent = send.at[k, 0 : (devices - 1) * chunk_rows, :]
        pltpu.make_async_copy(sent, sent, send_sems.at[k]).wait()
        return 0

    lax.fori_loop(0, chunks, drain, 0)


def shards(records, coords, bins, slow_index):
    ch_dev, local_samples = records.shape
    hop = W // 2
    snaps = local_samples // hop
    chan_count = lax.axis_size("chan")
    tm_count = lax.axis_size("tm")
    devices = chan_count * tm_count
    channels = ch_dev * chan_count
    freq = bins.shape[0]
    per_dev = freq // devices
    chunks = math.gcd(per_dev, CHUNKS)
    tiles = snaps * ch_dev // LANES
    chunk_rows = 2 * per_dev * tiles // chunks
    columns = TURNS * 4 * tm_count * tiles
    kept = 8 * ((per_dev + 7) // 8)
    own = slow_index.shape[1] // tm_count
    scale = 1.0 / (channels * snaps * tm_count)
    vmem = pl.BlockSpec(memory_space=pltpu.VMEM)
    inner_angles = pltpu.VMEM((8, channels), jnp.float32)
    angles = pltpu.VMEM((REACH, channels), jnp.float32)
    power = pl.pallas_call(
        functools.partial(kernel, scale, tm_count, chan_count),
        out_shape=jax.ShapeDtypeStruct((tm_count, kept, own), jnp.float32),
        in_specs=[pl.BlockSpec(memory_space=pl.ANY)] * 4,
        out_specs=vmem,
        scratch_shapes=[
            pltpu.SMEM(bins.shape, jnp.int32),
            pltpu.VMEM(slow_index.shape, jnp.int32),
            pltpu.VMEM(coords.shape, jnp.int32),
            pltpu.VMEM(((snaps + 1) * ch_dev, hop), jnp.bfloat16),
            pltpu.VMEM((2 * freq // chunks, W), jnp.bfloat16),
            pltpu.VMEM((2 * freq * tiles // chunks, LANES), jnp.float32),
            pltpu.VMEM((chunks, devices * chunk_rows, LANES), jnp.bfloat16),
            pltpu.VMEM((chunks, devices, chunk_rows, LANES), jnp.bfloat16),
            pltpu.VMEM((16, LANES), jnp.bfloat16),
            pltpu.VMEM((chan_count, 16, LANES), jnp.bfloat16),
            pltpu.VMEM((2, channels), jnp.float32),
            pltpu.VMEM((columns, channels), jnp.bfloat16),
            pltpu.VMEM((columns, channels), jnp.bfloat16),
            inner_angles, inner_angles, angles, angles,
            pltpu.VMEM((4, SET, channels), jnp.bfloat16),
            pltpu.VMEM((4, columns, SET), jnp.float32),
            pltpu.VMEM((per_dev * POINTS, SET), jnp.float32),
            pltpu.VMEM((1, slow_index.shape[1]), jnp.int32),
            pltpu.VMEM((SET, slow_index.shape[1]), jnp.bfloat16),
            pltpu.VMEM((tm_count, kept, own), jnp.float32),
            pltpu.VMEM((tm_count, kept, own), jnp.float32),
            pltpu.SemaphoreType.DMA,
            pltpu.SemaphoreType.DMA((3,)),
            pltpu.SemaphoreType.DMA((2,)),
            pltpu.SemaphoreType.DMA((2,)),
            pltpu.SemaphoreType.DMA((chunks,)),
            pltpu.SemaphoreType.DMA((chunks,)),
            pltpu.SemaphoreType.DMA((2, tm_count)),
        ],
        compiler_params=pltpu.CompilerParams(
            collective_id=0, has_side_effects=True, vmem_limit_bytes=63 * 2**20
        ),
        cost_estimate=pl.CostEstimate(
            flops=8 * SET * columns * channels * per_dev,
            bytes_accessed=records.size * 2,
            transcendentals=0,
        ),
    )(bins, slow_index, coords, records)
    return power[:, :per_dev, :].reshape(tm_count * per_dev, own).T


def solution(mesh):
    return jax.shard_map(
        shards,
        mesh=mesh,
        in_specs=(P("chan", "tm"), P(None, "chan"), P(), P()),
        out_specs=P("tm", "chan"),
        check_vma=False,
    )
```

```python
import functools
import math

import jax
import jax.numpy as jnp
import numpy as np
from jax import lax
from jax.experimental import pallas as pl
from jax.experimental.pallas import tpu as pltpu
from jax.sharding import PartitionSpec as P

W = 2048
REACH = 32
LANES = 128
INNER = 6
OUTER = 2
SPAN = 2 * INNER + 1
TURNS = 2 * OUTER + 1
CHUNKS = 3


def circle_fit():
    u = 0.125 * (1.0 - np.cos(math.pi * (np.arange(400) + 0.5) / 400))
    t = np.sqrt(u)
    powers = u[:, None] ** np.arange(6)[None, :]
    scaled = powers * (4.0 ** np.arange(6))
    cos_fit = np.linalg.lstsq(scaled, np.cos(2 * math.pi * t), rcond=None)[0]
    sin_fit = np.linalg.lstsq(scaled, np.sin(2 * math.pi * t) / t, rcond=None)[0]
    back = 4.0 ** np.arange(6)
    return [float(v) for v in cos_fit * back], [float(v) for v in sin_fit * back]


COS_FIT, SIN_FIT = circle_fit()


def horner(u, fit):
    total = jnp.full_like(u, fit[-1])
    for value in fit[-2::-1]:
        total = total * u + value
    return total


def circle(t):
    t = t - jnp.floor(t + 0.5)
    u = t * t
    return horner(u, COS_FIT), t * horner(u, SIN_FIT)


SECOND = INNER * REACH
FIRST = SECOND + REACH
SET = 2 * LANES
POINTS = 8 * ((4 * TURNS + 7) // 8)


def grid_place(slow_index):
    first, second = slow_index[0:1, :], slow_index[1:2, :]
    turn = sum((first + REACH >= SPAN * h).astype(jnp.int32) for h in range(1, TURNS))
    inner = first - SPAN * (turn - OUTER)
    low0, low1 = (inner < 0).astype(jnp.int32), (second < 0).astype(jnp.int32)
    a0, a1 = jnp.abs(inner), jnp.abs(second)
    quad = jnp.where(low0 == low1, low0, 2 + low0)
    quad = jnp.where(a0 == 0, low1, jnp.where(a1 == 0, low0, quad))
    lane = jnp.where(a0 == 0, SECOND + a1 - 1, (a0 - 1) * REACH + a1 - 1)
    return turn * 4 + quad, jnp.where(a1 == 0, FIRST + a0, lane)


def product(rows, columns):
    return lax.dot_general(
        rows, columns, (((1,), (1,)), ((), ())), preferred_element_type=jnp.float32
    )


def kernel(
    scale, sizes, tm_count, chan_count, bins_in, slow_in, coords_in, records_ref, out_ref,
    bins_ref, slow_ref, coords_ref,
    blocks, table, stage, send, recv, digits, all_digits, positions,
    yt, yj, c0, s0, c1, s1, sets, dots, power, place, onehot, mine, swapped,
    load_sem, small_sems, halo_sems, digit_sems, send_sems, recv_sems, power_sems,
):
    devices = tm_count * chan_count
    chunks = len(sizes)
    begins = [sum(sizes[:k]) for k in range(chunks)]
    ch_dev, local_samples = records_ref.shape
    hop = W // 2
    snaps = local_samples // hop
    tiles = snaps * ch_dev // LANES
    per_dev = bins_ref.shape[0] // devices
    bin_rows = 2 * tiles
    half = LANES // 2
    side = tm_count * 2 * tiles
    my_chan, my_tm = lax.axis_index("chan"), lax.axis_index("tm")
    me = my_chan * tm_count + my_tm
    lane = lax.broadcasted_iota(jnp.int32, (1, LANES), 1)
    mesh_id = pl.DeviceIdType.MESH

    barrier = pltpu.get_barrier_semaphore()

    def greet(j, _):
        other = lax.rem(me + j, devices)
        pl.semaphore_signal(
            barrier,
            inc=1,
            device_id=(lax.div(other, tm_count), lax.rem(other, tm_count)),
            device_id_type=mesh_id,
        )
        return 0

    lax.fori_loop(1, devices, greet, 0)

    small = [
        pltpu.make_async_copy(source, target, small_sems.at[i])
        for i, (source, target) in enumerate(
            ((coords_in, coords_ref), (bins_in, bins_ref), (slow_in, slow_ref))
        )
    ]
    for copy in small:
        copy.start()

    def load(n, _):
        pltpu.make_async_copy(
            records_ref.at[:, pl.ds(pl.multiple_of(n * hop, hop), hop)],
            blocks.at[pl.ds(pl.multiple_of(n * ch_dev, ch_dev), ch_dev), :],
            load_sem,
        ).start()
        return 0

    lax.fori_loop(0, snaps, load, 0)
    digits[...] = jnp.zeros_like(digits)
    for copy in small:
        copy.wait()
    for axis in range(2):
        values = coords_ref[axis : axis + 1, :].astype(jnp.float32)
        high = jnp.floor(values * (1.0 / 32.0))
        digits[2 * axis : 2 * axis + 1, 0:ch_dev] = high.astype(digits.dtype)
        digits[2 * axis + 1 : 2 * axis + 2, 0:ch_dev] = (values - 32.0 * high).astype(digits.dtype)
    all_digits[my_chan] = digits[...]
    pl.semaphore_wait(barrier, devices - 1)

    halo = pltpu.make_async_remote_copy(
        src_ref=records_ref.at[:, 0:hop],
        dst_ref=blocks.at[snaps * ch_dev : (snaps + 1) * ch_dev, :],
        send_sem=halo_sems.at[0],
        recv_sem=halo_sems.at[1],
        device_id=(my_chan, lax.rem(my_tm + tm_count - 1, tm_count)),
        device_id_type=mesh_id,
    )
    halo.start()

    def tell(j, _):
        pltpu.make_async_remote_copy(
            src_ref=digits,
            dst_ref=all_digits.at[my_chan],
            send_sem=digit_sems.at[0],
            recv_sem=digit_sems.at[1],
            device_id=(lax.rem(my_chan + j, chan_count), my_tm),
            device_id_type=mesh_id,
        ).start()
        return 0

    lax.fori_loop(1, chan_count, tell, 0)

    offset = lax.broadcasted_iota(jnp.int32, (1, W), 1).astype(jnp.float32) * (1.0 / W)
    weight = (0.5 - 0.5 * circle(offset)[0]) * math.sqrt(8.0 / (3.0 * W))
    row16 = lax.broadcasted_iota(jnp.int32, (16, 1), 0)
    quarter = lax.rem(row16, 2).astype(jnp.float32) * 0.25

    def table_chunk(k):
        def table_rows(r, _):
            values = jnp.zeros((16, 1), jnp.float32)
            for i in range(8):
                b = r * 8 + i
                index = lax.div(b, sizes[k]) * per_dev + begins[k] + lax.rem(b, sizes[k])
                values = jnp.where(row16 // 2 == i, bins_ref[index].astype(jnp.float32), values)
            turn = values * offset + quarter
            turn = turn - jnp.floor(turn + 0.5)
            rows = pl.ds(pl.multiple_of(r * 16, 16), 16)
            table[rows, :] = (weight * horner(turn * turn, COS_FIT)).astype(table.dtype)
            return 0

        lax.fori_loop(0, 2 * devices * sizes[k] // 16, table_rows, 0)

    table_chunk(0)
    whole = blocks.at[0 : snaps * ch_dev, :]
    pltpu.make_async_copy(whole, whole, load_sem).wait()

    def part(k, d, base=True):
        start = devices * begins[k] * bin_rows if base else 0
        rows = sizes[k] * bin_rows
        return pl.ds(pl.multiple_of(start + d * rows, bin_rows), rows)

    def partner(j):
        if devices & (devices - 1):
            return lax.rem(me + j, devices)
        other = me
        for b in range(devices.bit_length() - 1):
            flip = 1 - 2 * lax.rem(lax.div(me, 2**b), 2)
            other = other + lax.rem(lax.div(j, 2**b), 2) * flip * 2**b
        return other

    def send_chunk(k):
        freq_rows = 2 * devices * sizes[k]

        def transform(i, _):
            @pl.when(i == (tiles // 2 - 1 if k == 0 else -1))
            def _():
                halo.wait()
                tail = blocks[snaps * ch_dev :, :]
                last = my_tm == tm_count - 1
                blocks[snaps * ch_dev :, :] = jnp.where(last, jnp.zeros_like(tail), tail)

            start = pl.multiple_of(i * 2 * LANES, 2 * LANES)
            here = blocks[pl.ds(start, 2 * LANES), :]
            after = blocks[pl.ds(start + ch_dev, 2 * LANES), :]
            out = product(table[:freq_rows, :hop], here)
            out += product(table[:freq_rows, hop:], after)
            for j in range(2):
                rows = pl.ds(2 * i + j, freq_rows, stride=tiles)
                stage[rows, :] = out[:, j * LANES : (j + 1) * LANES]
            return 0

        lax.fori_loop(0, tiles // 2, transform, 0)

        def pack(d, _):
            send[part(k, d), :] = stage[part(k, d, False), :].astype(send.dtype)
            return 0

        lax.fori_loop(0, devices, pack, 0)

        def send_one(j, _):
            other = partner(j // 2 + lax.rem(j, 2) * (devices // 2))
            pltpu.make_async_remote_copy(
                src_ref=send.at[part(k, other), :],
                dst_ref=recv.at[part(k, me), :],
                send_sem=send_sems.at[k],
                recv_sem=recv_sems.at[k],
                device_id=(lax.div(other, tm_count), lax.rem(other, tm_count)),
                device_id_type=mesh_id,
            ).start()
            return 0

        lax.fori_loop(1, devices, send_one, 0)
        recv[part(k, me), :] = send[part(k, me), :]
        if k + 1 < chunks:
            table_chunk(k + 1)

    for k in range(chunks):
        send_chunk(k)

    point, spot = grid_place(slow_ref[...])
    place[...] = point
    for first in range(0, SET, 16):
        row = lax.broadcasted_iota(jnp.int32, (16, 1), 0) + first
        onehot[first : first + 16, :] = (row == spot).astype(jnp.float32).astype(onehot.dtype)
    sets[...] = jnp.zeros_like(sets)
    power[...] = jnp.zeros_like(power)

    others = all_digits.at[0 : chan_count - 1]
    pltpu.make_async_copy(others, others, digit_sems.at[1]).wait()
    pltpu.make_async_copy(others, others, digit_sems.at[0]).wait()
    for m in range(chan_count // 2):
        left = all_digits[2 * m].astype(jnp.float32)
        right = pltpu.roll(all_digits[2 * m + 1].astype(jnp.float32), half, 1)
        both = jnp.where(lane < half, left, right)
        for axis in range(2):
            high, low = both[2 * axis : 2 * axis + 1], both[2 * axis + 1 : 2 * axis + 2]
            positions[axis : axis + 1, m * LANES : (m + 1) * LANES] = 32.0 * high + low

    modulus = 5 * W // 2
    inner_step = lax.broadcasted_iota(jnp.int32, (8, 1), 0)
    inner_step = jnp.where(inner_step <= INNER, inner_step, SPAN).astype(jnp.float32)
    step = (lax.broadcasted_iota(jnp.int32, (REACH, 1), 0) + 1).astype(jnp.float32)

    def one_bin(k, local, _):
        f = begins[k] + local
        bin_value = bins_ref[me * per_dev + f].astype(jnp.float32)
        for axis, steps, cos_ref, sin_ref in ((0, inner_step, c0, s0), (1, step, c1, s1)):
            turn = positions[axis : axis + 1, :] * bin_value
            turn = (turn - modulus * jnp.floor(turn * (1.0 / modulus))) * (1.0 / modulus)
            turn = turn - jnp.floor(turn + 0.5)
            cosine, sine = circle(turn * steps)
            cos_ref[...] = cosine
            sin_ref[...] = sine
        for m in range(chan_count // 2):
            cols = slice(m * LANES, (m + 1) * LANES)
            cos_1, sin_1 = c0[INNER + 1 : INNER + 2, cols], s0[INNER + 1 : INNER + 2, cols]
            spins = [(cos_1, sin_1), (2.0 * cos_1 * cos_1 - 1.0, 2.0 * sin_1 * cos_1)]
            for t in range(tm_count):
                pairs = []
                for p in range(2):
                    start = devices * begins[k] * bin_rows + (2 * local + p) * tiles
                    start = pl.multiple_of(start, tiles)
                    step_rows = sizes[k] * bin_rows
                    source = 2 * m * tm_count + t
                    left = recv[pl.ds(start + source * step_rows, tiles), :].astype(jnp.float32)
                    source += tm_count
                    right = recv[pl.ds(start + source * step_rows, tiles), :].astype(jnp.float32)
                    even = jnp.where(lane < half, left, pltpu.roll(right, half, 1))
                    odd = jnp.where(lane < half, pltpu.roll(left, half, 1), right)
                    pairs.append((even, odd))
                for parity in range(2):
                    re, im = pairs[0][parity], pairs[1][parity]
                    turned = [None] * TURNS
                    turned[OUTER] = (re, im)
                    for h, (cosine, sine) in enumerate(spins, 1):
                        cr, si, ci, sr = cosine * re, sine * im, cosine * im, sine * re
                        turned[OUTER + h] = (cr + si, ci - sr)
                        turned[OUTER - h] = (cr - si, ci + sr)
                    for h, (real, imag) in enumerate(turned):
                        top = 2 * side * h + (t * 2 + parity) * tiles
                        low = top + side
                        yt[top : top + tiles, cols] = real.astype(yt.dtype)
                        yt[low : low + tiles, cols] = imag.astype(yt.dtype)
                        yj[top : top + tiles, cols] = imag.astype(yj.dtype)
                        yj[low : low + tiles, cols] = (-real).astype(yj.dtype)

        cosines, sines = c1[...], s1[...]
        for l in range(INNER):
            cos_row, sin_row = c0[l + 1 : l + 2, :], s0[l + 1 : l + 2, :]
            rows = slice(l * REACH, (l + 1) * REACH)
            sets[0, rows, :] = (cos_row * cosines).astype(sets.dtype)
            sets[1, rows, :] = (sin_row * sines).astype(sets.dtype)
            sets[2, rows, :] = (sin_row * cosines).astype(sets.dtype)
            sets[3, rows, :] = (cos_row * sines).astype(sets.dtype)
        sets[0, SECOND:FIRST, :] = cosines.astype(sets.dtype)
        sets[3, SECOND:FIRST, :] = sines.astype(sets.dtype)
        flat = slice(FIRST, FIRST + 16)
        sets[0, flat, :] = jnp.concatenate([c0[...]] * 2, axis=0).astype(sets.dtype)
        sets[2, flat, :] = jnp.concatenate([s0[...]] * 2, axis=0).astype(sets.dtype)
        for q in range(4):
            dots[q] = product((yt if q < 2 else yj)[...], sets[q])
        for h in range(TURNS):
            rows = slice(2 * side * h, 2 * side * (h + 1))
            cc, ss, sc, cs = dots[0, rows, :], dots[1, rows, :], dots[2, rows, :], dots[3, rows, :]
            even_same, even_other = cc - ss, cc + ss
            odd_same, odd_other = sc + cs, sc - cs
            for q, value in enumerate(
                (even_same + odd_same, even_same - odd_same, even_other + odd_other, even_other - odd_other)
            ):
                total = jnp.sum(value * value, axis=0, keepdims=True)
                power[pl.ds(f * POINTS + 4 * h + q, 1), :] = total * scale
        return 0

    def all_but_one(k):
        start = devices * begins[k] * bin_rows
        return pl.ds(start, (devices - 1) * sizes[k] * bin_rows)

    for k in range(chunks):
        arrived = recv.at[all_but_one(k), :]
        pltpu.make_async_copy(arrived, arrived, recv_sems.at[k]).wait()
        lax.fori_loop(0, sizes[k], functools.partial(one_bin, k), 0)

    high = power[...].astype(jnp.bfloat16)
    rest = (power[...] - high.astype(jnp.float32)).astype(jnp.bfloat16)
    point_row = lax.broadcasted_iota(jnp.int32, (POINTS, 1), 0)
    own = mine.shape[2]
    for t in range(tm_count):
        cols = slice(t * own, (t + 1) * own)
        spread = jnp.dot(high, onehot[:, cols], preferred_element_type=jnp.float32)
        spread += jnp.dot(rest, onehot[:, cols], preferred_element_type=jnp.float32)
        here = point_row == place[:, cols]
        for f in range(per_dev):
            rows = spread[f * POINTS : (f + 1) * POINTS]
            mine[t, f : f + 1, :] = jnp.sum(jnp.where(here, rows, 0.0), axis=0, keepdims=True)
    exchanges = []
    for j in range(1, tm_count):
        other = lax.rem(my_tm + j, tm_count)
        copy = pltpu.make_async_remote_copy(
            src_ref=mine.at[other],
            dst_ref=swapped.at[my_tm],
            send_sem=power_sems.at[0, j - 1],
            recv_sem=power_sems.at[1, j - 1],
            device_id=(my_chan, other),
            device_id_type=mesh_id,
        )
        copy.start()
        exchanges.append(copy)
    swapped[my_tm] = mine[my_tm]
    for copy in exchanges:
        copy.wait()
    out_ref[...] = swapped[...]

    for k in range(chunks):
        sent = send.at[all_but_one(k), :]
        pltpu.make_async_copy(sent, sent, send_sems.at[k]).wait()


def shards(records, coords, bins, slow_index):
    ch_dev, local_samples = records.shape
    hop = W // 2
    snaps = local_samples // hop
    chan_count = lax.axis_size("chan")
    tm_count = lax.axis_size("tm")
    devices = chan_count * tm_count
    channels = ch_dev * chan_count
    freq = bins.shape[0]
    per_dev = freq // devices
    chunks = min(per_dev, CHUNKS)
    sizes = tuple((per_dev + chunks - 1 - k) // chunks for k in range(chunks))
    tiles = snaps * ch_dev // LANES
    most = 2 * devices * max(sizes)
    columns = TURNS * 4 * tm_count * tiles
    kept = 8 * ((per_dev + 7) // 8)
    own = slow_index.shape[1] // tm_count
    scale = 1.0 / (channels * snaps * tm_count)
    vmem = pl.BlockSpec(memory_space=pltpu.VMEM)
    inner_angles = pltpu.VMEM((8, channels), jnp.float32)
    angles = pltpu.VMEM((REACH, channels), jnp.float32)
    power = pl.pallas_call(
        functools.partial(kernel, scale, sizes, tm_count, chan_count),
        out_shape=jax.ShapeDtypeStruct((tm_count, kept, own), jnp.float32),
        in_specs=[pl.BlockSpec(memory_space=pl.ANY)] * 4,
        out_specs=vmem,
        scratch_shapes=[
            pltpu.SMEM(bins.shape, jnp.int32),
            pltpu.VMEM(slow_index.shape, jnp.int32),
            pltpu.VMEM(coords.shape, jnp.int32),
            pltpu.VMEM(((snaps + 1) * ch_dev, hop), jnp.bfloat16),
            pltpu.VMEM((most, W), jnp.bfloat16),
            pltpu.VMEM((most * tiles, LANES), jnp.float32),
            pltpu.VMEM((2 * freq * tiles, LANES), jnp.bfloat16),
            pltpu.VMEM((2 * freq * tiles, LANES), jnp.bfloat16),
            pltpu.VMEM((16, LANES), jnp.bfloat16),
            pltpu.VMEM((chan_count, 16, LANES), jnp.bfloat16),
            pltpu.VMEM((2, channels), jnp.float32),
            pltpu.VMEM((columns, channels), jnp.bfloat16),
            pltpu.VMEM((columns, channels), jnp.bfloat16),
            inner_angles, inner_angles, angles, angles,
            pltpu.VMEM((4, SET, channels), jnp.bfloat16),
            pltpu.VMEM((4, columns, SET), jnp.float32),
            pltpu.VMEM((per_dev * POINTS, SET), jnp.float32),
            pltpu.VMEM((1, slow_index.shape[1]), jnp.int32),
            pltpu.VMEM((SET, slow_index.shape[1]), jnp.bfloat16),
            pltpu.VMEM((tm_count, kept, own), jnp.float32),
            pltpu.VMEM((tm_count, kept, own), jnp.float32),
            pltpu.SemaphoreType.DMA,
            pltpu.SemaphoreType.DMA((3,)),
            pltpu.SemaphoreType.DMA((2,)),
            pltpu.SemaphoreType.DMA((2,)),
            pltpu.SemaphoreType.DMA((chunks,)),
            pltpu.SemaphoreType.DMA((chunks,)),
            pltpu.SemaphoreType.DMA((2, tm_count)),
        ],
        compiler_params=pltpu.CompilerParams(
            collective_id=0, has_side_effects=True, vmem_limit_bytes=63 * 2**20
        ),
        cost_estimate=pl.CostEstimate(
            flops=8 * SET * columns * channels * per_dev,
            bytes_accessed=records.size * 2,
            transcendentals=0,
        ),
    )(bins, slow_index, coords, records)
    return power[:, :per_dev, :].reshape(tm_count * per_dev, own).T


def solution(mesh):
    return jax.shard_map(
        shards,
        mesh=mesh,
        in_specs=(P("chan", "tm"), P(None, "chan"), P(), P()),
        out_specs=P("tm", "chan"),
        check_vma=False,
    )
```
